128 devices in a mesh: row: 32 (over y, z, core), col: 4 (over x).
Axes of the slice: x: 4, y: 4, z: 4, core: 2. Of those that a mesh axis runs over, the one named last changes fastest.
Arguments:
- coupling: float32 [4096, 61440], P('row', 'col'), may hold values from 0.1 to 10
- src_left: bfloat16 [4096, 128], P('row'), may hold values from -8 to 8
- emitter_distance_rightside: bfloat16 [4096, 128], P('row'), may hold values from -0.09375 to 0.09375
- destination_distance_leftside: bfloat16 [128, 61440], P('row', 'col'), may hold values from -2 to 2
- tgt_right: bfloat16 [128, 61440], P('row', 'col'), may hold values from -0.0234375 to 0.0234375
- log_src: float32 [4096], P('row'), may hold values from -1 to 1
- logarithm_destination_masses: float32 [61440], P('col'), may hold values from -1 to 1
- tgt_potential: float32 [61440], P('col'), may hold values from -12 to 12
Outputs:
- refreshed_plan_matrix: float32 [4096, 61440], P('row', 'col')
- row_potential: float32 [4096], P('row')
- col_potential: float32 [61440], P('col')
The draws below stay inside these ranges and needn't reach their ends.
All inputs are finite; a program needn't handle non-finite values.
Results may differ from the reference program's by a relative error of at most 0.035.
The reference program's roundings to bfloat16 on the way count: a program that leaves them out, or rounds other values in their place, can miss the bound.
Values may be sent and summed in bfloat16 or wider, within the bound.
A program may use at most 64 MiB of HBM per device.

```python
import math
import jax
import jax.numpy as jnp
from jax import lax

K = 128
NS = 4096
NT = 61440


def draw_src_left(key, part):
    key = jax.random.fold_in(key, 11)
    key_common, key_own = jax.random.split(key, 2)
    shared_term = 1.9 * jnp.clip(jax.random.normal(key_common, (1, K), jnp.float32), -2.5, 2.5)
    own = 0.6 * jnp.clip(jax.random.normal(key_own, (NS, K), jnp.float32), -3.0, 3.0)
    return (shared_term + own).astype(jnp.bfloat16)


def draw_destination_distance_leftside(key, part):
    key = jax.random.fold_in(key, 23)
    key_common, key_own = jax.random.split(key, 2)
    shared_term = 0.28 * jnp.clip(jax.random.normal(key_common, (K, 1), jnp.float32), -3.0, 3.0)
    own = jnp.clip(jax.random.normal(key_own, (K, NT), jnp.float32), -4.0, 4.0) / math.sqrt(K)
    return (shared_term + own).astype(jnp.bfloat16)


def level_of(own_key, extent, shards, smallest, high):
    factor_of = 1.0
    for axis_at, blocks in shards:
        draws = jax.random.uniform(jax.random.fold_in(jax.random.fold_in(own_key, 6), axis_at), (blocks,), jnp.float32, smallest / len(shards), high / len(shards))
        factor_of = factor_of * jnp.repeat(jnp.exp(draws), extent[axis_at] // blocks).reshape((-1,) + (1,) * (len(extent) - 1 - axis_at))
    return factor_of


def noise(own_key, extent, scale, reach, shards=(), kind=jnp.bfloat16):
    entries = scale * jax.random.normal(own_key, extent, jnp.float32)
    if shards:
        entries = entries * level_of(own_key, extent, shards, -0.22, 0.18)
    return jnp.clip(entries, -reach, reach).astype(kind)


def setup_inputs(seed: int = 0) -> dict:
    arg_keys = jax.random.split(jax.random.key(seed), 9)
    coupling = jnp.clip(jnp.exp(math.log(10.0) - 4.6051702 * jax.random.uniform(arg_keys[0], (NS, NT), jnp.float32) ** level_of(arg_keys[0], (NS, NT), ((0, 32), (1, 4)), -0.2, 0.2)), 0.1, 10.0)
    src_left = draw_src_left(jax.random.fold_in(arg_keys[8], 71), 0)
    emitter_distance_rightside = noise(arg_keys[2], (NS, K), NS ** -0.5, 0.09375, ((0, 32),))
    destination_distance_leftside = draw_destination_distance_leftside(jax.random.fold_in(arg_keys[8], 71), 0)
    tgt_right = noise(arg_keys[4], (K, NT), NT ** -0.5, 0.0234375, ((0, 32), (1, 4)))
    log_src = jnp.clip(jax.random.uniform(arg_keys[5], (NS,), jnp.float32, -1.0, 1.0) * level_of(arg_keys[5], (NS,), ((0, 32),), -0.4, 0.0), -1.0, 1.0)
    logarithm_destination_masses = jnp.clip(jax.random.uniform(arg_keys[6], (NT,), jnp.float32, -1.0, 1.0) * level_of(arg_keys[6], (NT,), ((0, 4),), -0.4, 0.0), -1.0, 1.0)
    tgt_potential = noise(arg_keys[7], (NT,), 2.0, 12.0, ((0, 4),), jnp.float32)
    return {"coupling": coupling, "src_left": src_left, "emitter_distance_rightside": emitter_distance_rightside, "destination_distance_leftside": destination_distance_leftside, "tgt_right": tgt_right, "log_src": log_src, "logarithm_destination_masses": logarithm_destination_masses, "tgt_potential": tgt_potential}


regularization_strength = 4.0


def reference(coupling, src_left, emitter_distance_rightside, destination_distance_leftside, tgt_right, log_src, logarithm_destination_masses, tgt_potential):
    highest = lax.Precision.HIGHEST
    carried = lax.dot_general(coupling, tgt_right.astype(jnp.float32), (((1,), (1,)), ((), ())), precision=highest)
    rank_core = lax.dot_general(emitter_distance_rightside.astype(jnp.float32), carried, (((0,), (0,)), ((), ())), precision=highest)
    half_core_product = rank_core.astype(jnp.bfloat16)
    price_matrix_slab = jnp.dot(src_left, half_core_product, preferred_element_type=jnp.float32).astype(jnp.bfloat16)
    divided_price_matrix = jnp.dot(price_matrix_slab, destination_distance_leftside, preferred_element_type=jnp.float32) * (-2.0 / regularization_strength)
    row_potential = log_src - jax.nn.logsumexp(tgt_potential[None, :] - divided_price_matrix, axis=1)
    col_potential = logarithm_destination_masses - jax.nn.logsumexp(row_potential[:, None] - divided_price_matrix, axis=0)
    refreshed_plan_matrix = NS * jnp.exp(row_potential[:, None] + col_potential[None, :] - divided_price_matrix)
    return refreshed_plan_matrix, row_potential, col_potential
```

```python
import functools
import math

import jax
import jax.numpy as jnp
from jax import lax
from jax.experimental import pallas as pl
from jax.experimental.pallas import tpu as pltpu
from jax.sharding import PartitionSpec as P

MESH = pl.DeviceIdType.MESH
BF16 = jnp.bfloat16
F32 = jnp.float32
SIDE = 4
SHARE = 4
LANES = 128
REGULARIZATION = 4.0
LOG2E = math.log2(math.e)
LN2 = math.log(2.0)
SCORE = 2.0 / REGULARIZATION * LOG2E


def wrap(v):
    return lax.rem(v + 2 * SIDE, SIDE)


class Place:
    def __init__(self):
        row = lax.axis_index("row")
        self.x = lax.axis_index("col")
        self.y = lax.div(row, 2 * SIDE)
        self.z = lax.rem(lax.div(row, 2), SIDE)
        self.c = lax.rem(row, 2)

    def other(self, dx=0, dy=0, dz=0, dc=0):
        core = 1 - self.c if dc else self.c
        row = (wrap(self.y + dy) * SIDE + wrap(self.z + dz)) * 2 + core
        return {"row": row, "col": wrap(self.x + dx)}


class Gather:
    def __init__(self, here, raw, send, recv):
        self.here, self.raw, self.send, self.recv = here, raw, send, recv
        columns = raw.shape[-1]
        self.half, self.quarter = columns // 2, columns // 4
        self.copies = []

    def columns(self, kind, part):
        start = 0 if kind == "A" else self.half
        if part is None:
            return pl.ds(start, self.half)
        return pl.ds(start + part * self.quarter, self.quarter)

    def slot(self, kind, a, b, part):
        dy, dz = (a, b) if kind == "A" else (b, a)
        h = self.here
        return self.raw.at[wrap(h.y + dy), wrap(h.z + dz), h.c, :, self.columns(kind, part)]

    def target(self, kind, which, step):
        first = which == "first"
        along_z = first == (kind == "A")
        return self.here.other(dz=step) if along_z else self.here.other(dy=step)

    def copy(self, index, ref, device):
        return pltpu.make_async_remote_copy(
            src_ref=ref,
            dst_ref=ref,
            send_sem=self.send.at[index],
            recv_sem=self.recv.at[index],
            device_id=device,
            device_id_type=MESH,
        )

    def start(self, kind, number, a, b, part, which, step):
        base = 0 if kind == "A" else 24
        device = self.target(kind, which, step)
        copy = self.copy(base + number, self.slot(kind, a, b, part), device)
        copy.start()
        self.copies.append(copy)

    def arrived(self, kind, number, a, b, part):
        base = 0 if kind == "A" else 24
        copy = self.copy(base + number, self.slot(kind, a, b, part), self.here.other(dc=1))
        copy.wait_recv()

    def line(self, kind, number, a):
        h = self.here
        if kind == "A":
            ref = self.raw.at[wrap(h.y + a), :, h.c, :, self.columns(kind, None)]
        else:
            ref = self.raw.at[:, wrap(h.z + a), h.c, :, self.columns(kind, None)]
        base = 0 if kind == "A" else 24
        copy = self.copy(base + 20 + number, ref, h.other(dc=1))
        copy.start()
        self.copies.append(copy)

    def own(self):
        for kind in "AB":
            self.start(kind, 0, 0, 0, None, "first", 1)
            self.start(kind, 1, 0, 0, None, "first", -1)
        for kind in "AB":
            self.start(kind, 2, 0, 0, None, "last", 1)
            self.start(kind, 3, 0, 0, None, "last", -1)

    def first(self):
        for kind in "AB":
            self.arrived(kind, 0, 0, -1, None)
            self.start(kind, 4, 0, -1, 0, "first", 1)
            self.start(kind, 6, 0, -1, None, "last", 1)
            self.start(kind, 7, 0, -1, None, "last", -1)
            self.arrived(kind, 1, 0, 1, None)
            self.start(kind, 5, 0, 1, 1, "first", -1)
            self.start(kind, 8, 0, 1, None, "last", 1)
            self.start(kind, 9, 0, 1, None, "last", -1)

    def first_last(self):
        for kind in "AB":
            self.arrived(kind, 2, -1, 0, None)
            self.start(kind, 12, -1, 0, 0, "last", 1)
            self.arrived(kind, 3, 1, 0, None)
            self.start(kind, 16, 1, 0, 1, "last", -1)

    def second(self):
        for kind in "AB":
            self.arrived(kind, 4, 0, 2, 0)
            self.arrived(kind, 5, 0, 2, 1)
            self.start(kind, 10, 0, 2, None, "last", 1)
            self.start(kind, 11, 0, 2, None, "last", -1)
            self.line(kind, 0, 0)

    def second_last(self):
        for kind in "AB":
            for k, b in ((0, -1), (1, 1)):
                self.arrived(kind, 6 + 2 * k, -1, b, None)
                self.start(kind, 13 + k, -1, b, 0, "last", 1)
                self.arrived(kind, 7 + 2 * k, 1, b, None)
                self.start(kind, 17 + k, 1, b, 1, "last", -1)

    def third(self):
        for kind in "AB":
            self.arrived(kind, 10, -1, 2, None)
            self.start(kind, 15, -1, 2, 0, "last", 1)
            self.line(kind, 1, -1)
            self.arrived(kind, 11, 1, 2, None)
            self.start(kind, 19, 1, 2, 1, "last", -1)
            self.line(kind, 2, 1)

    def fourth(self):
        for kind in "AB":
            for k, b in enumerate((0, -1, 1, 2)):
                self.arrived(kind, 12 + k, 2, b, 0)
                self.arrived(kind, 16 + k, 2, b, 1)
            self.line(kind, 3, 2)

    def siblings(self):
        h = self.here
        for kind in "AB":
            base = 0 if kind == "A" else 24
            for number, a in enumerate((0, -1, 1, 2)):
                if kind == "A":
                    ref = self.raw.at[wrap(h.y + a), :, 1 - h.c, :, self.columns(kind, None)]
                else:
                    ref = self.raw.at[:, wrap(h.z + a), 1 - h.c, :, self.columns(kind, None)]
                self.copy(base + 20 + number, ref, h.other(dc=1)).wait_recv()

    def finish(self):
        for copy in self.copies:
            copy.wait_send()


class Exchange:
    def __init__(self, here, buffer, send, recv, axis):
        self.here, self.buffer, self.send, self.recv, self.axis = here, buffer, send, recv, axis
        self.me = getattr(here, axis)

    def copies(self):
        for k, step in enumerate((1, -1, 2)):
            ref = self.buffer.at[self.me]
            yield pltpu.make_async_remote_copy(
                src_ref=ref,
                dst_ref=ref,
                send_sem=self.send.at[k],
                recv_sem=self.recv.at[k],
                device_id=self.here.other(**{"d" + self.axis: step}),
                device_id_type=MESH,
            )

    def start(self):
        for copy in self.copies():
            copy.start()

    def wait(self):
        for k, step in enumerate((1, -1, 2)):
            ref = self.buffer.at[wrap(self.me - step)]
            pltpu.make_async_remote_copy(
                src_ref=ref,
                dst_ref=ref,
                send_sem=self.send.at[k],
                recv_sem=self.recv.at[k],
                device_id=self.here.other(dc=1),
                device_id_type=MESH,
            ).wait_recv()

    def finish(self):
        for copy in self.copies():
            copy.wait_send()


def to_sibling(here, src, dst, send, recv, index):
    return pltpu.make_async_remote_copy(
        src_ref=src,
        dst_ref=dst,
        send_sem=send.at[index],
        recv_sem=recv.at[index],
        device_id=here.other(dc=1),
        device_id_type=MESH,
    )


def added(parts):
    return (parts[0] + parts[1]) + (parts[2] + parts[3])


def merged(parts):
    peak = functools.reduce(jnp.maximum, parts)
    total = functools.reduce(jnp.add, [jnp.exp2(part - peak) for part in parts])
    return peak + jnp.log2(total)


def step_of(columns, most):
    return max(s for s in range(LANES, most + 1, LANES) if columns % s == 0)


def main_kernel(
    coupling_hbm, tgt_right_hbm, tgt_left_hbm,
    src_left, src_right, log_src, log_tgt, tgt_potential,
    left_out, rows_out, row_shift_out, row_out, col_out,
    raw_right, raw_left, wide, image, whole_left, core_part, core_sib, core_x, core_y, core_z, core_half,
    peaks, totals, row_parts, col_all, col_sib, col_z, col_y, image_acc,
    local, right_send, right_recv, left_send, left_recv,
    small_send, small_recv, sib_send, sib_recv,
):
    here = Place()
    columns = wide.shape[1]
    rows = wide.shape[0]

    own_right = pltpu.make_async_copy(tgt_right_hbm, raw_right.at[here.y, here.z, here.c], local.at[0])
    own_left = pltpu.make_async_copy(tgt_left_hbm, raw_left.at[here.y, here.z, here.c], local.at[1])
    own_right.start()
    own_left.start()
    load = pltpu.make_async_copy(coupling_hbm, wide, local.at[2])
    load.start()

    barrier = pltpu.get_barrier_semaphore()
    partners = [here.other(dc=1)]
    for axis in "xyz":
        partners += [here.other(**{"d" + axis: step}) for step in (1, -1, 2)]
    for partner in partners:
        pl.semaphore_signal(barrier, inc=1, device_id=partner, device_id_type=MESH)
    own_right.wait()
    own_left.wait()
    pl.semaphore_wait(barrier, len(partners))

    right = Gather(here, raw_right, right_send, right_recv)
    left = Gather(here, raw_left, left_send, left_recv)
    right.own()

    side = src_right[...].astype(F32).T.astype(BF16)
    width = step_of(columns, 512)

    def image_step(i, _):
        at = pl.ds(pl.multiple_of(i * width, width), width)
        entries = wide[:, at]
        high = entries.astype(BF16)
        low = (entries - high.astype(F32)).astype(BF16)
        value = jnp.dot(side, high, preferred_element_type=F32) + jnp.dot(side, low, preferred_element_type=F32)
        value_high = value.astype(BF16)
        image[0:rows, at] = value_high
        image[rows : 2 * rows, at] = (value - value_high.astype(F32)).astype(BF16)
        return 0

    steps = columns // width
    cut_one, cut_two = steps // 4, (steps * 5) // 8
    load.wait()
    lax.fori_loop(0, cut_one, image_step, 0)
    right.first()
    right.first_last()
    left.own()
    lax.fori_loop(cut_one, cut_two, image_step, 0)
    right.second()
    lax.fori_loop(cut_two, steps, image_step, 0)
    right.second_last()
    right.third()
    left.first()
    left.first_last()
    right.fourth()
    right.siblings()

    image_acc[...] = jnp.zeros_like(image_acc)
    span = step_of(columns, 3072)

    def core_step(i, _):
        at = pl.ds(pl.multiple_of(i * span, span), span)
        factor = raw_right[:, :, :, :, at].reshape(LANES, span)
        image_acc[...] += lax.dot_general(
            image[:, at], factor, (((1,), (1,)), ((), ())), preferred_element_type=F32
        )
        return 0

    lax.fori_loop(0, columns // span, core_step, 0)
    core_part[...] = image_acc[0:LANES] + image_acc[LANES : 2 * LANES]

    part_rows = LANES // 2
    mine = pl.ds(pl.multiple_of(here.c * part_rows, part_rows), part_rows)
    theirs = pl.ds(pl.multiple_of((1 - here.c) * part_rows, part_rows), part_rows)
    core_swap = to_sibling(here, core_part.at[theirs], core_sib, sib_send, sib_recv, 0)
    core_swap.start()
    left.second()
    core_swap.wait_recv()
    core_x[here.x] = core_part[mine] + core_sib[...]
    sum_x = Exchange(here, core_x, small_send.at[0], small_recv.at[0], "x")
    sum_x.start()
    left.second_last()
    sum_x.wait()
    core_y[here.y] = added([core_x[k] for k in range(SIDE)])
    sum_y = Exchange(here, core_y, small_send.at[1], small_recv.at[1], "y")
    sum_y.start()
    left.third()
    sum_y.wait()
    core_z[here.z] = added([core_y[k] for k in range(SIDE)])
    sum_z = Exchange(here, core_z, small_send.at[2], small_recv.at[2], "z")
    sum_z.start()
    left.fourth()
    sum_z.wait()
    core_half[here.c] = added([core_z[k] for k in range(SIDE)]).astype(BF16)
    half_swap = to_sibling(here, core_half.at[here.c], core_half.at[here.c], sib_send, sib_recv, 1)
    half_swap.start()
    to_sibling(here, core_half.at[1 - here.c], core_half.at[1 - here.c], sib_send, sib_recv, 1).wait_recv()
    core = core_half[...].reshape(LANES, LANES)
    rows_cost = jnp.dot(src_left[...], core, preferred_element_type=F32).astype(BF16)
    rows_out[...] = rows_cost
    left.siblings()

    peaks[...] = jnp.full_like(peaks, -jnp.inf)
    reach = step_of(columns, 1024)
    tiles = reach // LANES

    def score_step(i, _):
        at = pl.ds(pl.multiple_of(i * reach, reach), reach)
        factor = raw_left[:, :, :, :, at].reshape(LANES, reach)
        whole_left[:, at] = factor
        score = jnp.dot(rows_out[...], factor, preferred_element_type=F32) * SCORE
        wide[:, at] = score
        peak = peaks[...]
        for q in range(tiles):
            shift = tgt_potential[pl.ds(i * tiles + q, 1), :] * LOG2E
            peak = jnp.maximum(peak, score[:, q * LANES : (q + 1) * LANES] + shift)
        peaks[...] = peak
        return 0

    lax.fori_loop(0, columns // reach, score_step, 0)
    save = pltpu.make_async_copy(whole_left, left_out, local.at[3])
    save.start()

    totals[...] = jnp.zeros_like(totals)

    def total_step(i, _):
        peak = peaks[...]
        total = totals[...]
        for q in range(tiles):
            at = pl.ds(pl.multiple_of(i * reach + q * LANES, LANES), LANES)
            shift = tgt_potential[pl.ds(i * tiles + q, 1), :] * LOG2E
            total = total + jnp.exp2(wide[:, at] + shift - peak)
        totals[...] = total
        return 0

    lax.fori_loop(0, columns // reach, total_step, 0)
    lane_peak = peaks[...].T
    row_peak = jnp.max(lane_peak, axis=0, keepdims=True)
    row_total = jnp.sum(totals[...].T * jnp.exp2(lane_peak - row_peak), axis=0, keepdims=True)
    row_parts[here.x] = jnp.broadcast_to(row_peak + jnp.log2(row_total), row_parts.shape[1:])
    rows_x = Exchange(here, row_parts, small_send.at[3], small_recv.at[3], "x")
    rows_x.start()
    rows_x.wait()
    row_sum = merged([row_parts[k] for k in range(SIDE)])[0:1]
    row_potential = log_src[...] - LN2 * row_sum
    row_out[...] = row_potential
    row_shift_out[...] = jnp.broadcast_to(row_potential * LOG2E, (LANES, LANES)).T

    def col_step(i, _):
        shift = row_shift_out[...]
        for q in range(tiles):
            at = pl.ds(pl.multiple_of(i * reach + q * LANES, LANES), LANES)
            score = wide[:, at] + shift
            peak = jnp.max(score, axis=0, keepdims=True)
            total = jnp.sum(jnp.exp2(score - peak), axis=0, keepdims=True)
            col_all[pl.ds(i * tiles + q, 1), :] = peak + jnp.log2(total)
        return 0

    lax.fori_loop(0, columns // reach, col_step, 0)

    col_rows = col_all.shape[0]
    some = col_sib.shape[0]
    rest = col_rows - some
    mine = pl.ds(pl.multiple_of(here.c * rest, 8), some)
    theirs = pl.ds(pl.multiple_of((1 - here.c) * rest, 8), some)
    col_swap = to_sibling(here, col_all.at[theirs], col_sib, sib_send, sib_recv, 2)
    col_swap.start()
    col_swap.wait_recv()
    col_z[here.z] = merged([col_all[mine, :], col_sib[...]])
    sum_z2 = Exchange(here, col_z, small_send.at[4], small_recv.at[4], "z")
    sum_z2.start()
    sum_z2.wait()
    col_y[here.y] = merged([col_z[k] for k in range(SIDE)])
    sum_y2 = Exchange(here, col_y, small_send.at[5], small_recv.at[5], "y")
    sum_y2.start()
    sum_y2.wait()
    col_out[mine, :] = log_tgt[mine, :] - LN2 * merged([col_y[k] for k in range(SIDE)])
    sent = pl.ds(pl.multiple_of(here.c * some, 8), rest)
    taken = pl.ds(pl.multiple_of((1 - here.c) * some, 8), rest)
    col_share = to_sibling(here, col_out.at[sent], col_out.at[sent], sib_send, sib_recv, 3)
    col_share.start()
    to_sibling(here, col_out.at[taken], col_out.at[taken], sib_send, sib_recv, 3).wait_recv()

    save.wait()
    right.finish()
    left.finish()
    for exchange in (sum_x, sum_y, sum_z, rows_x, sum_z2, sum_y2):
        exchange.finish()
    for copy in (core_swap, half_swap, col_swap, col_share):
        copy.wait_send()


def plan_kernel(source_count, rows_cost, row_shift, row_in, col_in, left, plan, row_out, col_out):
    i = pl.program_id(0)
    row_out[...] = row_in[...]
    tiles = plan.shape[1] // LANES
    score = jnp.dot(rows_cost[...], left[...], preferred_element_type=F32) * SCORE
    shift = row_shift[...]
    for q in range(tiles):
        here = pl.ds(i * tiles + q, 1)
        potential = col_in[here, :]
        col_out[here, :] = potential
        part = score[:, q * LANES : (q + 1) * LANES] + shift
        plan[:, q * LANES : (q + 1) * LANES] = jnp.exp2(part + (potential * LOG2E + math.log2(source_count)))


def per_device(
    coupling,
    src_left,
    emitter_distance_rightside,
    destination_distance_leftside,
    tgt_right,
    log_src,
    logarithm_destination_masses,
    tgt_potential,
):
    rows, columns = coupling.shape
    rank = src_left.shape[1]
    col_rows = columns // LANES
    some = -(-col_rows // 16) * 8
    source_count = rows * lax.axis_size("row")
    blocks = (SIDE, SIDE, 2, SHARE, columns)
    vmem = pl.BlockSpec(memory_space=pltpu.VMEM)
    anywhere = pl.BlockSpec(memory_space=pl.ANY)
    left, rows_cost, row_shift, row_potential, col_potential = pl.pallas_call(
        main_kernel,
        name="main",
        out_shape=[
            jax.ShapeDtypeStruct((rank, columns), BF16),
            jax.ShapeDtypeStruct((rows, rank), BF16),
            jax.ShapeDtypeStruct((rows, LANES), F32),
            jax.ShapeDtypeStruct((1, rows), F32),
            jax.ShapeDtypeStruct((col_rows, LANES), F32),
        ],
        in_specs=[anywhere] * 3 + [vmem] * 5,
        out_specs=[anywhere] + [vmem] * 4,
        scratch_shapes=[
            pltpu.VMEM(blocks, BF16),
            pltpu.VMEM(blocks, BF16),
            pltpu.VMEM((rows, columns), F32),
            pltpu.VMEM((2 * rank, columns), BF16),
            pltpu.VMEM((rank, columns), BF16),
            pltpu.VMEM((rank, rank), F32),
            pltpu.VMEM((rank // 2, rank), F32),
            pltpu.VMEM((SIDE, rank // 2, rank), F32),
            pltpu.VMEM((SIDE, rank // 2, rank), F32),
            pltpu.VMEM((SIDE, rank // 2, rank), F32),
            pltpu.VMEM((2, rank // 2, rank), BF16),
            pltpu.VMEM((rows, LANES), F32),
            pltpu.VMEM((rows, LANES), F32),
            pltpu.VMEM((SIDE, 8, LANES), F32),
            pltpu.VMEM((col_rows, LANES), F32),
            pltpu.VMEM((some, LANES), F32),
            pltpu.VMEM((SIDE, some, LANES), F32),
            pltpu.VMEM((SIDE, some, LANES), F32),
            pltpu.VMEM((2 * rank, rank), F32),
            pltpu.SemaphoreType.DMA((4,)),
            pltpu.SemaphoreType.DMA((48,)),
            pltpu.SemaphoreType.DMA((48,)),
            pltpu.SemaphoreType.DMA((48,)),
            pltpu.SemaphoreType.DMA((48,)),
            pltpu.SemaphoreType.DMA((6, 3)),
            pltpu.SemaphoreType.DMA((6, 3)),
            pltpu.SemaphoreType.DMA((4,)),
            pltpu.SemaphoreType.DMA((4,)),
        ],
        compiler_params=pltpu.CompilerParams(
            collective_id=0, has_side_effects=True, vmem_limit_bytes=56 * 1024 * 1024
        ),
    )(
        coupling,
        tgt_right,
        destination_distance_leftside,
        src_left,
        emitter_distance_rightside,
        log_src.reshape(1, rows),
        logarithm_destination_masses.reshape(col_rows, LANES),
        tgt_potential.reshape(col_rows, LANES),
    )
    width = step_of(columns, 1536)
    whole = lambda *shape: pl.BlockSpec(shape, lambda i: (0,) * len(shape))
    plan, row_potential, col_potential = pl.pallas_call(
        functools.partial(plan_kernel, source_count),
        name="plan",
        grid=(columns // width,),
        out_shape=[
            jax.ShapeDtypeStruct((rows, columns), F32),
            jax.ShapeDtypeStruct((1, rows), F32),
            jax.ShapeDtypeStruct((col_rows, LANES), F32),
        ],
        in_specs=[
            whole(rows, rank),
            whole(rows, LANES),
            whole(1, rows),
            whole(col_rows, LANES),
            pl.BlockSpec((rank, width), lambda i: (0, i)),
        ],
        out_specs=[pl.BlockSpec((rows, width), lambda i: (0, i)), whole(1, rows), whole(col_rows, LANES)],
        compiler_params=pltpu.CompilerParams(vmem_limit_bytes=32 * 1024 * 1024),
    )(rows_cost, row_shift, row_potential, col_potential, left)
    return plan, row_potential.reshape(rows), col_potential.reshape(columns)


def solution(mesh):
    return jax.shard_map(
        per_device,
        mesh=mesh,
        in_specs=(
            P("row", "col"),
            P("row", None),
            P("row", None),
            P("row", "col"),
            P("row", "col"),
            P("row"),
            P("col"),
            P("col"),
        ),
        out_specs=(P("row", "col"), P("row"), P("col")),
        check_vma=False,
    )
```

```python
import functools
import math

import jax
import jax.numpy as jnp
from jax import lax
from jax.experimental import pallas as pl
from jax.experimental.pallas import tpu as pltpu
from jax.sharding import PartitionSpec as P

MESH = pl.DeviceIdType.MESH
BF16 = jnp.bfloat16
F32 = jnp.float32
SIDE = 4
SHARE = 4
LANES = 128
REGULARIZATION = 4.0
LOG2E = math.log2(math.e)
LN2 = math.log(2.0)
SCORE = 2.0 / REGULARIZATION * LOG2E


def wrap(v):
    return lax.rem(v + 2 * SIDE, SIDE)


class Place:
    def __init__(self):
        row = lax.axis_index("row")
        self.x = lax.axis_index("col")
        self.y = lax.div(row, 2 * SIDE)
        self.z = lax.rem(lax.div(row, 2), SIDE)
        self.c = lax.rem(row, 2)

    def other(self, dx=0, dy=0, dz=0, dc=0):
        core = 1 - self.c if dc else self.c
        row = (wrap(self.y + dy) * SIDE + wrap(self.z + dz)) * 2 + core
        return {"row": row, "col": wrap(self.x + dx)}


class Gather:
    KINDS = ("A", "B")
    MESSAGES = 37

    def __init__(self, here, raw, send, recv):
        self.here, self.raw, self.send, self.recv = here, raw, send, recv
        columns = raw.shape[-1]
        self.half, self.quarter = columns // 2, columns // 4
        self.started = []

    def ref(self, kind, a, b, part, core=None):
        h = self.here
        core = h.c if core is None else core
        start = 0 if kind == "A" else self.half
        if part is None:
            columns = pl.ds(start, self.half)
        else:
            columns = pl.ds(start + part * self.quarter, self.quarter)
        dy, dz = (a, b) if kind == "A" else (b, a)
        y = slice(None) if dy is None else wrap(h.y + dy)
        z = slice(None) if dz is None else wrap(h.z + dz)
        return self.raw.at[y, z, core, :, columns]

    def copy(self, kind, number, ref, device):
        index = number + (0 if kind == "A" else self.MESSAGES)
        return pltpu.make_async_remote_copy(
            src_ref=ref,
            dst_ref=ref,
            send_sem=self.send.at[index],
            recv_sem=self.recv.at[index],
            device_id=device,
            device_id_type=MESH,
        )

    def start(self, kind, number, ref, device):
        copy = self.copy(kind, number, ref, device)
        copy.start()
        self.started.append(copy)

    def wait(self, kind, number, ref):
        self.copy(kind, number, ref, self.here.other(dc=1)).wait_recv()

    def along(self, kind, first, step):
        if first == (kind == "A"):
            return self.here.other(dz=step)
        return self.here.other(dy=step)


    @staticmethod
    def side(step):
        return 0 if step == 1 else 1

    def first_number(self, part, step):
        return part * 2 + self.side(step)

    def last_number(self, b, part, step):
        return 6 + (b + 1) * 4 + part * 2 + self.side(step)

    def on_number(self, b, step):
        return 22 + (b + 1) * 2 + self.side(step)

    def first(self, kind, part, step):
        self.start(kind, self.first_number(part, step), self.ref(kind, 0, 0, part), self.along(kind, True, step))

    def wait_first(self, kind, part, step):
        self.wait(kind, self.first_number(part, step), self.ref(kind, 0, -step, part))

    def first_on(self, kind, step):
        part = self.side(step)
        self.start(kind, 4 + part, self.ref(kind, 0, -step, part), self.along(kind, True, step))

    def wait_first_on(self, kind, step):
        part = self.side(step)
        self.wait(kind, 4 + part, self.ref(kind, 0, 2, part))

    def last(self, kind, b, part, step):
        self.start(kind, self.last_number(b, part, step), self.ref(kind, 0, b, part), self.along(kind, False, step))

    def wait_last(self, kind, b, part, step):
        self.wait(kind, self.last_number(b, part, step), self.ref(kind, -step, b, part))

    def last_on(self, kind, b, step):
        part = self.side(step)
        self.start(kind, self.on_number(b, step), self.ref(kind, -step, b, part), self.along(kind, False, step))

    def wait_last_on(self, kind, b, step):
        part = self.side(step)
        self.wait(kind, self.on_number(b, step), self.ref(kind, 2, b, part))

    def to_sibling(self, kind, number, a, b):
        self.start(kind, 30 + number, self.ref(kind, a, b, None), self.here.other(dc=1))

    def wait_sibling(self, kind, number, a, b):
        self.wait(kind, 30 + number, self.ref(kind, a, b, None, 1 - self.here.c))

    STEPS = ((1, 0), (-1, 1))

    def step(self, number):
        getattr(self, "step_%d" % number)()

    def step_0(self):
        for kind in self.KINDS:
            for step, part in self.STEPS:
                self.first(kind, part, step)
        for kind in self.KINDS:
            for step, part in self.STEPS:
                self.first(kind, 1 - part, step)
        for kind in self.KINDS:
            for step, part in self.STEPS:
                self.last(kind, 0, part, step)
        for kind in self.KINDS:
            for step, part in self.STEPS:
                self.last(kind, 0, 1 - part, step)

    def step_1(self):
        for kind in self.KINDS:
            for step, part in self.STEPS:
                self.wait_first(kind, part, step)
                self.first_on(kind, step)
                self.last(kind, -step, part, step)

    def step_2(self):
        for kind in self.KINDS:
            for step, part in self.STEPS:
                self.wait_first(kind, 1 - part, step)
                self.last(kind, -step, 1 - part, -step)

    def step_3(self):
        for kind in self.KINDS:
            for step, part in self.STEPS:
                self.wait_last(kind, 0, part, step)
                self.last_on(kind, 0, step)
        for kind in self.KINDS:
            for b in (-1, 1):
                for step, part in self.STEPS:
                    self.last(kind, b, 1 - part, step)

    def step_4(self):
        for kind in self.KINDS:
            for step, part in self.STEPS:
                self.wait_first_on(kind, step)
                self.last(kind, 2, part, step)
        for kind in self.KINDS:
            self.to_sibling(kind, 0, 0, None)

    def step_5(self):
        for kind in self.KINDS:
            for b in (-1, 1):
                for step, part in self.STEPS:
                    self.wait_last(kind, b, part, step)
                    self.last_on(kind, b, step)
        for kind in self.KINDS:
            for step, part in self.STEPS:
                self.last(kind, 2, 1 - part, step)

    def step_6(self):
        for kind in self.KINDS:
            for step, part in self.STEPS:
                self.wait_last(kind, 2, part, step)
                self.last_on(kind, 2, step)

    def step_7(self):
        for kind in self.KINDS:
            for step, part in self.STEPS:
                for b in (0, -1, 1, 2):
                    self.wait_last(kind, b, 1 - part, step)
                self.to_sibling(kind, 1 + part, -step, None)

    def step_8(self):
        for k, b in enumerate((0, -1, 1, 2)):
            for kind in self.KINDS:
                for step, part in self.STEPS:
                    self.wait_last_on(kind, b, step)
                self.to_sibling(kind, 3 + k, 2, b)

    def step_9(self):
        for kind in self.KINDS:
            for k, a in enumerate((0, -1, 1)):
                self.wait_sibling(kind, k, a, None)
            for k, b in enumerate((0, -1, 1, 2)):
                self.wait_sibling(kind, 3 + k, 2, b)

    def finish(self):
        for copy in self.started:
            copy.wait_send()


class Exchange:
    def __init__(self, here, buffer, send, recv, axis):
        self.here, self.buffer, self.send, self.recv, self.axis = here, buffer, send, recv, axis
        self.me = getattr(here, axis)

    def copies(self):
        for k, step in enumerate((1, -1, 2)):
            ref = self.buffer.at[self.me]
            yield pltpu.make_async_remote_copy(
                src_ref=ref,
                dst_ref=ref,
                send_sem=self.send.at[k],
                recv_sem=self.recv.at[k],
                device_id=self.here.other(**{"d" + self.axis: step}),
                device_id_type=MESH,
            )

    def start(self):
        for copy in self.copies():
            copy.start()

    def wait(self):
        for k, step in enumerate((1, -1, 2)):
            ref = self.buffer.at[wrap(self.me - step)]
            pltpu.make_async_remote_copy(
                src_ref=ref,
                dst_ref=ref,
                send_sem=self.send.at[k],
                recv_sem=self.recv.at[k],
                device_id=self.here.other(dc=1),
                device_id_type=MESH,
            ).wait_recv()

    def finish(self):
        for copy in self.copies():
            copy.wait_send()


def to_sibling(here, src, dst, send, recv, index):
    return pltpu.make_async_remote_copy(
        src_ref=src,
        dst_ref=dst,
        send_sem=send.at[index],
        recv_sem=recv.at[index],
        device_id=here.other(dc=1),
        device_id_type=MESH,
    )


def added(parts):
    return (parts[0] + parts[1]) + (parts[2] + parts[3])


def merged(parts):
    peak = functools.reduce(jnp.maximum, parts)
    total = functools.reduce(jnp.add, [jnp.exp2(part - peak) for part in parts])
    return peak + jnp.log2(total)


def step_of(columns, most):
    return max(s for s in range(LANES, most + 1, LANES) if columns % s == 0)


def main_kernel(
    coupling_hbm, tgt_right_hbm, tgt_left_hbm,
    src_left_hbm, src_right_hbm, log_src_hbm, log_tgt_hbm, tgt_potential_hbm,
    wide, row_shift_out, row_out, col_out,
    raw_right, raw_left, image, core_part, core_sib, core_x, core_y, core_z, core_half,
    peaks, totals, row_parts, col_all, col_sib, col_z, col_y, image_acc,
    src_left, src_right, log_src, log_tgt, tgt_potential,
    local, right_send, right_recv, left_send, left_recv,
    small_send, small_recv, sib_send, sib_recv,
):
    here = Place()
    columns = wide.shape[1]
    rows = wide.shape[0]

    loads = []
    for k, (source, target) in enumerate((
        (tgt_right_hbm, raw_right.at[here.y, here.z, here.c]),
        (src_right_hbm, src_right),
        (tgt_left_hbm, raw_left.at[here.y, here.z, here.c]),
        (coupling_hbm, wide),
        (src_left_hbm, src_left),
        (log_src_hbm, log_src),
        (log_tgt_hbm, log_tgt),
        (tgt_potential_hbm, tgt_potential),
    )):
        loads.append(pltpu.make_async_copy(source, target, local.at[k]))
        loads[-1].start()

    barrier = pltpu.get_barrier_semaphore()
    partners = [here.other(dc=1)]
    for axis in "xyz":
        partners += [here.other(**{"d" + axis: step}) for step in (1, -1, 2)]
    for partner in partners:
        pl.semaphore_signal(barrier, inc=1, device_id=partner, device_id_type=MESH)
    loads[0].wait()
    pl.semaphore_wait(barrier, len(partners))

    right = Gather(here, raw_right, right_send, right_recv)
    left = Gather(here, raw_left, left_send, left_recv)
    right.step(0)

    for k in (1, 2, 3):
        loads[k].wait()
    side = src_right[...].astype(F32).T.astype(BF16)
    side = jnp.concatenate([side, side], axis=1)
    width = step_of(columns, 3072)

    def image_step(i, _):
        at = pl.ds(pl.multiple_of(i * width, width), width)
        entries = wide[:, at]
        high = entries.astype(BF16)
        low = (entries - high.astype(F32)).astype(BF16)
        value = jnp.dot(side, jnp.concatenate([high, low], axis=0), preferred_element_type=F32)
        value_high = value.astype(BF16)
        image[0:LANES, at] = value_high
        image[LANES : 2 * LANES, at] = (value - value_high.astype(F32)).astype(BF16)
        return 0

    steps = columns // width
    cuts = [0] + [(steps * (k + 2)) // 5 for k in range(3)] + [steps]
    for k in range(4):
        lax.fori_loop(cuts[k], cuts[k + 1], image_step, 0)
        right.step(k + 1)
    right.step(5)
    right.step(6)
    left.step(0)
    right.step(7)
    right.step(8)
    left.step(1)
    left.step(2)
    right.step(9)

    image_acc[...] = jnp.zeros_like(image_acc)
    span = step_of(columns, 5120)

    def core_step(i, _):
        at = pl.ds(pl.multiple_of(i * span, span), span)
        factor = raw_right[:, :, :, :, at].reshape(LANES, span)
        image_acc[...] += lax.dot_general(
            image[:, at], factor, (((1,), (1,)), ((), ())), preferred_element_type=F32
        )
        return 0

    lax.fori_loop(0, columns // span, core_step, 0)
    core_part[...] = image_acc[0:LANES] + image_acc[LANES : 2 * LANES]

    part_rows = LANES // 2
    mine = pl.ds(pl.multiple_of(here.c * part_rows, part_rows), part_rows)
    theirs = pl.ds(pl.multiple_of((1 - here.c) * part_rows, part_rows), part_rows)
    core_swap = to_sibling(here, core_part.at[theirs], core_sib, sib_send, sib_recv, 0)
    core_swap.start()
    left.step(3)
    core_swap.wait_recv()
    core_x[here.x] = core_part[mine] + core_sib[...]
    sum_x = Exchange(here, core_x, small_send.at[0], small_recv.at[0], "x")
    sum_x.start()
    left.step(4)
    left.step(5)
    sum_x.wait()
    core_y[here.y] = added([core_x[k] for k in range(SIDE)])
    sum_y = Exchange(here, core_y, small_send.at[1], small_recv.at[1], "y")
    sum_y.start()
    left.step(6)
    left.step(7)
    sum_y.wait()
    core_z[here.z] = added([core_y[k] for k in range(SIDE)])
    sum_z = Exchange(here, core_z, small_send.at[2], small_recv.at[2], "z")
    sum_z.start()
    left.step(8)
    sum_z.wait()
    core_half[here.c] = added([core_z[k] for k in range(SIDE)]).astype(BF16)
    half_swap = to_sibling(here, core_half.at[here.c], core_half.at[here.c], sib_send, sib_recv, 1)
    half_swap.start()
    for k in range(4, 8):
        loads[k].wait()
    left.step(9)
    to_sibling(here, core_half.at[1 - here.c], core_half.at[1 - here.c], sib_send, sib_recv, 1).wait_recv()
    core = core_half[...].reshape(LANES, LANES)
    rows_cost = jnp.dot(src_left[...], core, preferred_element_type=F32).astype(BF16)

    peaks[...] = jnp.full_like(peaks, -jnp.inf)
    tiles = span // LANES

    def score_step(i, _):
        at = pl.ds(pl.multiple_of(i * span, span), span)
        factor = raw_left[:, :, :, :, at].reshape(LANES, span)
        score = jnp.dot(rows_cost, factor, preferred_element_type=F32) * SCORE
        wide[:, at] = score
        peak = peaks[...]
        for q in range(tiles):
            shift = tgt_potential[pl.ds(i * tiles + q, 1), :] * LOG2E
            peak = jnp.maximum(peak, score[:, q * LANES : (q + 1) * LANES] + shift)
        peaks[...] = peak
        return 0

    lax.fori_loop(0, columns // span, score_step, 0)

    totals[...] = jnp.zeros_like(totals)
    reach = step_of(columns, 3072)
    pieces = reach // LANES

    def total_step(i, _):
        peak = peaks[...]
        total = totals[...]
        for q in range(pieces):
            at = pl.ds(pl.multiple_of(i * reach + q * LANES, LANES), LANES)
            shift = tgt_potential[pl.ds(i * pieces + q, 1), :] * LOG2E
            total = total + jnp.exp2(wide[:, at] + shift - peak)
        totals[...] = total
        return 0

    lax.fori_loop(0, columns // reach, total_step, 0)
    lane_peak = peaks[...].T
    row_peak = jnp.max(lane_peak, axis=0, keepdims=True)
    row_total = jnp.sum(totals[...].T * jnp.exp2(lane_peak - row_peak), axis=0, keepdims=True)
    row_parts[here.x] = jnp.broadcast_to(row_peak + jnp.log2(row_total), row_parts.shape[1:])
    rows_x = Exchange(here, row_parts, small_send.at[3], small_recv.at[3], "x")
    rows_x.start()
    rows_x.wait()
    row_sum = merged([row_parts[k] for k in range(SIDE)])[0:1]
    row_potential = log_src[...] - LN2 * row_sum
    row_out[...] = row_potential
    row_shift_out[...] = jnp.broadcast_to(row_potential * LOG2E, (LANES, LANES)).T

    def col_step(i, _):
        for q in range(pieces):
            at = pl.ds(pl.multiple_of(i * reach + q * LANES, LANES), LANES)
            score = (wide[:, at] + row_shift_out[...]).reshape(rows // 8, 8, LANES)
            peak = jnp.max(score, axis=0)
            total = jnp.sum(jnp.exp2(score - peak[None]), axis=0)
            top = jnp.max(peak, axis=0, keepdims=True)
            total = jnp.sum(total * jnp.exp2(peak - top), axis=0, keepdims=True)
            col_all[pl.ds(i * pieces + q, 1), :] = top + jnp.log2(total)
        return 0

    lax.fori_loop(0, columns // reach, col_step, 0)

    col_rows = col_all.shape[0]
    some = col_sib.shape[0]
    rest = col_rows - some
    mine = pl.ds(pl.multiple_of(here.c * rest, 8), some)
    theirs = pl.ds(pl.multiple_of((1 - here.c) * rest, 8), some)
    col_swap = to_sibling(here, col_all.at[theirs], col_sib, sib_send, sib_recv, 2)
    col_swap.start()
    col_swap.wait_recv()
    col_z[here.z] = merged([col_all[mine, :], col_sib[...]])
    sum_z2 = Exchange(here, col_z, small_send.at[4], small_recv.at[4], "z")
    sum_z2.start()
    sum_z2.wait()
    col_y[here.y] = merged([col_z[k] for k in range(SIDE)])
    sum_y2 = Exchange(here, col_y, small_send.at[5], small_recv.at[5], "y")
    sum_y2.start()
    right.finish()
    left.finish()
    sum_y2.wait()
    col_out[mine, :] = log_tgt[mine, :] - LN2 * merged([col_y[k] for k in range(SIDE)])
    sent = pl.ds(pl.multiple_of(here.c * some, 8), rest)
    taken = pl.ds(pl.multiple_of((1 - here.c) * some, 8), rest)
    col_share = to_sibling(here, col_out.at[sent], col_out.at[sent], sib_send, sib_recv, 3)
    col_share.start()
    to_sibling(here, col_out.at[taken], col_out.at[taken], sib_send, sib_recv, 3).wait_recv()

    for exchange in (sum_x, sum_y, sum_z, rows_x, sum_z2, sum_y2):
        exchange.finish()
    for copy in (core_swap, half_swap, col_swap, col_share):
        copy.wait_send()


def plan_kernel(source_count, score, row_shift, row_in, col_in, plan, row_out, col_out):
    i = pl.program_id(0)
    row_out[...] = row_in[...]
    width = plan.shape[1]
    tiles = width // LANES
    for q in range(tiles):
        piece = pl.ds(i * tiles + q, 1)
        potential = col_in[piece, :]
        col_out[piece, :] = potential
        at = pl.ds(pl.multiple_of(i * width + q * LANES, LANES), LANES)
        shift = potential * LOG2E + math.log2(source_count)
        plan[:, q * LANES : (q + 1) * LANES] = jnp.exp2(score[:, at] + row_shift[...] + shift)


def per_device(
    coupling,
    src_left,
    emitter_distance_rightside,
    destination_distance_leftside,
    tgt_right,
    log_src,
    logarithm_destination_masses,
    tgt_potential,
):
    rows, columns = coupling.shape
    rank = src_left.shape[1]
    col_rows = columns // LANES
    some = -(-col_rows // 16) * 8
    source_count = rows * lax.axis_size("row")
    blocks = (SIDE, SIDE, 2, SHARE, columns)
    vmem = pl.BlockSpec(memory_space=pltpu.VMEM)
    anywhere = pl.BlockSpec(memory_space=pl.ANY)
    inputs = [
        coupling,
        tgt_right,
        destination_distance_leftside,
        src_left,
        emitter_distance_rightside,
        log_src.reshape(1, rows),
        logarithm_destination_masses.reshape(col_rows, LANES),
        tgt_potential.reshape(col_rows, LANES),
    ]
    outputs = pl.pallas_call(
        main_kernel,
        name="main",
        out_shape=[
            pltpu.VMEM((rows, columns), F32),
            pltpu.VMEM((rows, LANES), F32),
            pltpu.VMEM((1, rows), F32),
            pltpu.VMEM((col_rows, LANES), F32),
        ],
        in_specs=[anywhere] * len(inputs),
        out_specs=[vmem] * 4,
        scratch_shapes=[
            pltpu.VMEM(blocks, BF16),
            pltpu.VMEM(blocks, BF16),
            pltpu.VMEM((2 * rank, columns), BF16),
            pltpu.VMEM((rank, rank), F32),
            pltpu.VMEM((rank // 2, rank), F32),
            pltpu.VMEM((SIDE, rank // 2, rank), F32),
            pltpu.VMEM((SIDE, rank // 2, rank), F32),
            pltpu.VMEM((SIDE, rank // 2, rank), F32),
            pltpu.VMEM((2, rank // 2, rank), BF16),
            pltpu.VMEM((rows, LANES), F32),
            pltpu.VMEM((rows, LANES), F32),
            pltpu.VMEM((SIDE, 8, LANES), F32),
            pltpu.VMEM((col_rows, LANES), F32),
            pltpu.VMEM((some, LANES), F32),
            pltpu.VMEM((SIDE, some, LANES), F32),
            pltpu.VMEM((SIDE, some, LANES), F32),
            pltpu.VMEM((2 * rank, rank), F32),
            pltpu.VMEM((rows, rank), BF16),
            pltpu.VMEM((rows, rank), BF16),
            pltpu.VMEM((1, rows), F32),
            pltpu.VMEM((col_rows, LANES), F32),
            pltpu.VMEM((col_rows, LANES), F32),
            pltpu.SemaphoreType.DMA((len(inputs),)),
            pltpu.SemaphoreType.DMA((2 * Gather.MESSAGES,)),
            pltpu.SemaphoreType.DMA((2 * Gather.MESSAGES,)),
            pltpu.SemaphoreType.DMA((2 * Gather.MESSAGES,)),
            pltpu.SemaphoreType.DMA((2 * Gather.MESSAGES,)),
            pltpu.SemaphoreType.DMA((6, 3)),
            pltpu.SemaphoreType.DMA((6, 3)),
            pltpu.SemaphoreType.DMA((4,)),
            pltpu.SemaphoreType.DMA((4,)),
        ],
        compiler_params=pltpu.CompilerParams(
            collective_id=0, has_side_effects=True, vmem_limit_bytes=44 * 1024 * 1024
        ),
    )(*[pltpu.with_memory_space_constraint(array, pltpu.HBM) for array in inputs])
    outputs = [pltpu.with_memory_space_constraint(array, pltpu.VMEM) for array in outputs]
    width = step_of(columns, 3072)
    whole = lambda *shape: pl.BlockSpec(shape, lambda i: (0,) * len(shape))
    plan, row_potential, col_potential = pl.pallas_call(
        functools.partial(plan_kernel, source_count),
        name="plan",
        grid=(columns // width,),
        out_shape=[
            jax.ShapeDtypeStruct((rows, columns), F32),
            jax.ShapeDtypeStruct((1, rows), F32),
            jax.ShapeDtypeStruct((col_rows, LANES), F32),
        ],
        in_specs=[vmem] * 4,
        out_specs=[pl.BlockSpec((rows, width), lambda i: (0, i)), whole(1, rows), whole(col_rows, LANES)],
        compiler_params=pltpu.CompilerParams(vmem_limit_bytes=32 * 1024 * 1024),
    )(*outputs)
    return plan, row_potential.reshape(rows), col_potential.reshape(columns)


def solution(mesh):
    return jax.shard_map(
        per_device,
        mesh=mesh,
        in_specs=(
            P("row", "col"),
            P("row", None),
            P("row", None),
            P("row", "col"),
            P("row", "col"),
            P("row"),
            P("col"),
            P("col"),
        ),
        out_specs=(P("row", "col"), P("row"), P("col")),
        check_vma=False,
    )
```

```python
import functools
import math

import jax
import jax.numpy as jnp
from jax import lax
from jax.experimental import pallas as pl
from jax.experimental.pallas import tpu as pltpu
from jax.sharding import PartitionSpec as P

MESH = pl.DeviceIdType.MESH
BF16 = jnp.bfloat16
F32 = jnp.float32
SIDE = 4
SHARE = 4
LANES = 128
REGULARIZATION = 4.0
LOG2E = math.log2(math.e)
LN2 = math.log(2.0)
SCORE = 2.0 / REGULARIZATION * LOG2E


def wrap(v):
    return lax.rem(v + 2 * SIDE, SIDE)


class Place:
    def __init__(self):
        row = lax.axis_index("row")
        self.x = lax.axis_index("col")
        self.y = lax.div(row, 2 * SIDE)
        self.z = lax.rem(lax.div(row, 2), SIDE)
        self.c = lax.rem(row, 2)
        self.near = {axis: {step: wrap(getattr(self, axis) + step) for step in (-1, 0, 1, 2)} for axis in "xyz"}
        self.ids = {}

    def other(self, dx=0, dy=0, dz=0, dc=0):
        key = (dx, dy, dz, dc)
        if key not in self.ids:
            core = 1 - self.c if dc else self.c
            row = (self.near["y"][dy] * SIDE + self.near["z"][dz]) * 2 + core
            self.ids[key] = {"row": row, "col": self.near["x"][dx]}
        return self.ids[key]


class Gather:
    KINDS = ("A", "B")
    RECEIVES = 41
    SENDS = 3

    def __init__(self, here, raw, send, recv):
        self.here, self.raw, self.send, self.recv = here, raw, send, recv
        columns = raw.shape[-1]
        self.half, self.quarter = columns // 2, columns // 4

    def ref(self, kind, a, b, part, core=None):
        h = self.here
        core = h.c if core is None else core
        start = 0 if kind == "A" else self.half
        if part is None:
            columns = pl.ds(start, self.half)
        else:
            columns = pl.ds(start + part * self.quarter, self.quarter)
        dy, dz = (a, b) if kind == "A" else (b, a)
        y = slice(None) if dy is None else h.near["y"][dy]
        z = slice(None) if dz is None else h.near["z"][dz]
        return self.raw.at[y, z, core, :, columns]


    def copy(self, send, receive, ref, device):
        return pltpu.make_async_remote_copy(
            src_ref=ref,
            dst_ref=ref,
            send_sem=self.send.at[send],
            recv_sem=self.recv.at[receive],
            device_id=device,
            device_id_type=MESH,
        )

    def start(self, send, receive, ref, device):
        self.copy(send, receive, ref, device).start()

    def wait(self, receive, ref):
        self.copy(0, receive, ref, self.here.other(dc=1)).wait_recv()

    def along(self, kind, first, step):
        if first == (kind == "A"):
            return self.here.other(dz=step)
        return self.here.other(dy=step)


    @staticmethod
    def side(step):
        return 0 if step == 1 else 1

    def number(self, kind, number):
        return number + (0 if kind == "A" else 20)

    def first_number(self, kind, part, step):
        return self.number(kind, part * 2 + self.side(step))

    def last_number(self, kind, b, part, step):
        ends = part != self.side(step)
        return self.number(kind, 14 + self.side(step) if ends else 8 + 2 * b + part)

    def first(self, kind, part, step):
        number = self.first_number(kind, part, step)
        self.start(0, number, self.ref(kind, 0, 0, part), self.along(kind, True, step))

    def wait_first(self, kind, part, step):
        self.wait(self.first_number(kind, part, step), self.ref(kind, 0, -step, part))

    def first_on(self, kind, step):
        part = self.side(step)
        self.start(0, self.number(kind, 4 + part), self.ref(kind, 0, -step, part), self.along(kind, True, step))

    def wait_first_on(self, kind, step):
        part = self.side(step)
        self.wait(self.number(kind, 4 + part), self.ref(kind, 0, 2, part))

    def last(self, kind, b, part, step):
        number = self.last_number(kind, b, part, step)
        self.start(1, number, self.ref(kind, 0, b, part), self.along(kind, False, step))

    def wait_last(self, kind, b, step):
        part = self.side(step)
        self.wait(self.last_number(kind, b, part, step), self.ref(kind, -step, b, part))

    def wait_ending(self, kind, step):
        part = 1 - self.side(step)
        self.wait(self.last_number(kind, 0, part, step), self.ref(kind, -step, None, part))

    def last_on(self, kind, b, step):
        part = self.side(step)
        self.start(1, self.number(kind, 17 + b), self.ref(kind, -step, b, part), self.along(kind, False, step))

    def wait_last_on(self, kind, b):
        self.wait(self.number(kind, 17 + b), self.ref(kind, 2, b, None))

    def to_sibling(self, kind, a, b):
        self.start(2, 40, self.ref(kind, a, b, None), self.here.other(dc=1))

    STEPS = ((1, 0), (-1, 1))

    def step(self, number):
        getattr(self, "step_%d" % number)()

    def step_0(self):
        for kind in self.KINDS:
            for step, part in self.STEPS:
                self.first(kind, part, step)
        for kind in self.KINDS:
            for step, part in self.STEPS:
                self.first(kind, 1 - part, step)
        for kind in self.KINDS:
            for step, part in self.STEPS:
                self.last(kind, 0, part, step)
        for kind in self.KINDS:
            for step, part in self.STEPS:
                self.last(kind, 0, 1 - part, step)

    def step_1(self):
        for kind in self.KINDS:
            for step, part in self.STEPS:
                self.wait_first(kind, part, step)
                self.first_on(kind, step)
                self.last(kind, -step, part, step)

    def step_2(self):
        for kind in self.KINDS:
            for step, part in self.STEPS:
                self.wait_first(kind, 1 - part, step)
                self.last(kind, -step, 1 - part, -step)

    def step_3(self):
        for kind in self.KINDS:
            for step, part in self.STEPS:
                self.wait_last(kind, 0, step)
                self.last_on(kind, 0, step)
        for kind in self.KINDS:
            for b in (-1, 1):
                for step, part in self.STEPS:
                    self.last(kind, b, 1 - part, step)

    def step_4(self):
        for kind in self.KINDS:
            for step, part in self.STEPS:
                self.wait_first_on(kind, step)
                self.last(kind, 2, part, step)
        for kind in self.KINDS:
            self.to_sibling(kind, 0, None)

    def step_5(self):
        for kind in self.KINDS:
            for b in (-1, 1):
                for step, part in self.STEPS:
                    self.wait_last(kind, b, step)
                    self.last_on(kind, b, step)
        for kind in self.KINDS:
            for step, part in self.STEPS:
                self.last(kind, 2, 1 - part, step)

    def step_6(self):
        for kind in self.KINDS:
            for step, part in self.STEPS:
                self.wait_last(kind, 2, step)
                self.last_on(kind, 2, step)

    def step_7(self):
        for kind in self.KINDS:
            for step, _ in self.STEPS:
                self.wait_ending(kind, step)
                self.to_sibling(kind, -step, None)

    def step_8(self):
        for b in (0, -1, 1, 2):
            for kind in self.KINDS:
                self.wait_last_on(kind, b)
                self.to_sibling(kind, 2, b)

    def step_9(self):
        self.wait(40, self.raw.at[:, :, 1 - self.here.c])

    def finish(self):
        for send, ref in enumerate((self.raw.at[0, 0:3, 0], self.raw.at[0:3, :, 0], self.raw.at[:, :, 0])):
            self.copy(send, 0, ref, self.here.other(dc=1)).wait_send()


class Exchange:
    def __init__(self, here, buffer, send, recv, number, axis):
        self.here, self.buffer, self.axis = here, buffer, axis
        self.send, self.recv = send.at[number], recv.at[number]

    def copy(self, ref, device):
        return pltpu.make_async_remote_copy(
            src_ref=ref,
            dst_ref=ref,
            send_sem=self.send,
            recv_sem=self.recv,
            device_id=device,
            device_id_type=MESH,
        )

    def start(self):
        for step in (2, 1, -1):
            own = self.buffer.at[getattr(self.here, self.axis)]
            self.copy(own, self.here.other(**{"d" + self.axis: step})).start()

    def wait(self):
        self.copy(self.buffer.at[0:3], self.here.other(dc=1)).wait_recv()

    def finish(self):
        self.copy(self.buffer.at[0:3], self.here.other(dc=1)).wait_send()


def to_sibling(here, src, dst, send, recv, index):
    return pltpu.make_async_remote_copy(
        src_ref=src,
        dst_ref=dst,
        send_sem=send.at[index],
        recv_sem=recv.at[index],
        device_id=here.other(dc=1),
        device_id_type=MESH,
    )


def added(parts):
    return (parts[0] + parts[1]) + (parts[2] + parts[3])


def merged(parts):
    peak = functools.reduce(jnp.maximum, parts)
    total = functools.reduce(jnp.add, [jnp.exp2(part - peak) for part in parts])
    return peak + jnp.log2(total)


def step_of(columns, most):
    return max(s for s in range(LANES, most + 1, LANES) if columns % s == 0)


def main_kernel(
    coupling_hbm, tgt_right_hbm, tgt_left_hbm,
    src_left_hbm, src_right_hbm, log_src_hbm, log_tgt_hbm, tgt_potential_hbm,
    wide, row_shift_out, row_out, col_out,
    raw_right, raw_left, image, core_part, core_sib, core_x, core_y, core_z, core_half,
    peaks, totals, row_parts, col_all, col_sib, col_z, col_y, image_acc,
    src_left, src_right, log_src, log_tgt, tgt_potential,
    local, right_send, right_recv, left_send, left_recv,
    small_send, small_recv, sib_send, sib_recv,
):
    here = Place()
    columns = wide.shape[1]
    rows = wide.shape[0]

    loads = []
    for k, (source, target) in enumerate((
        (tgt_right_hbm, raw_right.at[here.y, here.z, here.c]),
        (src_right_hbm, src_right),
        (tgt_left_hbm, raw_left.at[here.y, here.z, here.c]),
        (coupling_hbm, wide),
        (src_left_hbm, src_left),
        (log_src_hbm, log_src),
        (log_tgt_hbm, log_tgt),
        (tgt_potential_hbm, tgt_potential),
    )):
        loads.append(pltpu.make_async_copy(source, target, local.at[k]))
        loads[-1].start()

    barrier = pltpu.get_barrier_semaphore()
    partners = [here.other(dc=1)]
    for axis in "xyz":
        partners += [here.other(**{"d" + axis: step}) for step in (1, -1, 2)]
    for partner in partners:
        pl.semaphore_signal(barrier, inc=1, device_id=partner, device_id_type=MESH)
    loads[0].wait()
    pl.semaphore_wait(barrier, len(partners))

    right = Gather(here, raw_right, right_send, right_recv)
    left = Gather(here, raw_left, left_send, left_recv)
    right.step(0)

    for k in (1, 2, 3):
        loads[k].wait()
    side = src_right[...].astype(F32).T.astype(BF16)
    side = jnp.concatenate([side, side], axis=1)
    width = step_of(columns, 3072)

    def image_step(i, _):
        at = pl.ds(pl.multiple_of(i * width, width), width)
        entries = wide[:, at]
        high = entries.astype(BF16)
        low = (entries - high.astype(F32)).astype(BF16)
        value = jnp.dot(side, jnp.concatenate([high, low], axis=0), preferred_element_type=F32)
        value_high = value.astype(BF16)
        image[0:LANES, at] = value_high
        image[LANES : 2 * LANES, at] = (value - value_high.astype(F32)).astype(BF16)
        return 0

    steps = columns // width
    cuts = [0] + [(steps * (k + 2)) // 5 for k in range(3)] + [steps]
    for k in range(4):
        lax.fori_loop(cuts[k], cuts[k + 1], image_step, 0)
        right.step(k + 1)
    right.step(5)
    right.step(6)
    left.step(0)
    right.step(7)
    right.step(8)
    left.step(1)
    left.step(2)
    right.step(9)

    image_acc[...] = jnp.zeros_like(image_acc)
    span = step_of(columns, 5120)

    def core_step(i, _):
        at = pl.ds(pl.multiple_of(i * span, span), span)
        factor = raw_right[:, :, :, :, at].reshape(LANES, span)
        image_acc[...] += lax.dot_general(
            image[:, at], factor, (((1,), (1,)), ((), ())), preferred_element_type=F32
        )
        return 0

    lax.fori_loop(0, columns // span, core_step, 0)
    core_part[...] = image_acc[0:LANES] + image_acc[LANES : 2 * LANES]

    part_rows = LANES // 2
    mine = pl.ds(pl.multiple_of(here.c * part_rows, part_rows), part_rows)
    theirs = pl.ds(pl.multiple_of((1 - here.c) * part_rows, part_rows), part_rows)
    core_swap = to_sibling(here, core_part.at[theirs], core_sib, sib_send, sib_recv, 0)
    core_swap.start()
    left.step(3)
    core_swap.wait_recv()
    core_x[here.x] = core_part[mine] + core_sib[...]
    sum_x = Exchange(here, core_x, small_send, small_recv, 0, "x")
    sum_x.start()
    left.step(4)
    left.step(5)
    sum_x.wait()
    core_y[here.y] = added([core_x[k] for k in range(SIDE)])
    sum_y = Exchange(here, core_y, small_send, small_recv, 1, "y")
    sum_y.start()
    left.step(6)
    left.step(7)
    sum_y.wait()
    core_z[here.z] = added([core_y[k] for k in range(SIDE)])
    sum_z = Exchange(here, core_z, small_send, small_recv, 2, "z")
    sum_z.start()
    left.step(8)
    sum_z.wait()
    core_half[here.c] = added([core_z[k] for k in range(SIDE)]).astype(BF16)
    half_swap = to_sibling(here, core_half.at[here.c], core_half.at[here.c], sib_send, sib_recv, 1)
    half_swap.start()
    for k in range(4, 8):
        loads[k].wait()
    left.step(9)
    to_sibling(here, core_half.at[1 - here.c], core_half.at[1 - here.c], sib_send, sib_recv, 1).wait_recv()
    core = core_half[...].reshape(LANES, LANES)
    rows_cost = jnp.dot(src_left[...], core, preferred_element_type=F32).astype(BF16)

    peaks[...] = jnp.full_like(peaks, -jnp.inf)
    tiles = span // LANES

    def score_step(i, _):
        at = pl.ds(pl.multiple_of(i * span, span), span)
        factor = raw_left[:, :, :, :, at].reshape(LANES, span)
        score = jnp.dot(rows_cost, factor, preferred_element_type=F32) * SCORE
        wide[:, at] = score
        peak = peaks[...]
        for q in range(tiles):
            shift = tgt_potential[pl.ds(i * tiles + q, 1), :] * LOG2E
            peak = jnp.maximum(peak, score[:, q * LANES : (q + 1) * LANES] + shift)
        peaks[...] = peak
        return 0

    lax.fori_loop(0, columns // span, score_step, 0)

    totals[...] = jnp.zeros_like(totals)
    reach = step_of(columns, 3072)
    pieces = reach // LANES

    def total_step(i, _):
        peak = peaks[...]
        total = totals[...]
        for q in range(pieces):
            at = pl.ds(pl.multiple_of(i * reach + q * LANES, LANES), LANES)
            shift = tgt_potential[pl.ds(i * pieces + q, 1), :] * LOG2E
            total = total + jnp.exp2(wide[:, at] + shift - peak)
        totals[...] = total
        return 0

    lax.fori_loop(0, columns // reach, total_step, 0)
    lane_peak = peaks[...].T
    row_peak = jnp.max(lane_peak, axis=0, keepdims=True)
    row_total = jnp.sum(totals[...].T * jnp.exp2(lane_peak - row_peak), axis=0, keepdims=True)
    row_parts[here.x] = jnp.broadcast_to(row_peak + jnp.log2(row_total), row_parts.shape[1:])
    rows_x = Exchange(here, row_parts, small_send, small_recv, 3, "x")
    rows_x.start()
    rows_x.wait()
    row_sum = merged([row_parts[k] for k in range(SIDE)])[0:1]
    row_potential = log_src[...] - LN2 * row_sum
    row_out[...] = row_potential
    row_shift_out[...] = jnp.broadcast_to(row_potential * LOG2E, (LANES, LANES)).T

    def col_step(i, _):
        for q in range(pieces):
            at = pl.ds(pl.multiple_of(i * reach + q * LANES, LANES), LANES)
            score = (wide[:, at] + row_shift_out[...]).reshape(rows // 8, 8, LANES)
            peak = jnp.max(score, axis=0)
            total = jnp.sum(jnp.exp2(score - peak[None]), axis=0)
            top = jnp.max(peak, axis=0, keepdims=True)
            total = jnp.sum(total * jnp.exp2(peak - top), axis=0, keepdims=True)
            col_all[pl.ds(i * pieces + q, 1), :] = top + jnp.log2(total)
        return 0

    lax.fori_loop(0, columns // reach, col_step, 0)

    col_rows = col_all.shape[0]
    some = col_sib.shape[0]
    rest = col_rows - some
    mine = pl.ds(pl.multiple_of(here.c * rest, 8), some)
    theirs = pl.ds(pl.multiple_of((1 - here.c) * rest, 8), some)
    col_swap = to_sibling(here, col_all.at[theirs], col_sib, sib_send, sib_recv, 2)
    col_swap.start()
    col_swap.wait_recv()
    col_z[here.z] = merged([col_all[mine, :], col_sib[...]])
    sum_z2 = Exchange(here, col_z, small_send, small_recv, 4, "z")
    sum_z2.start()
    sum_z2.wait()
    col_y[here.y] = merged([col_z[k] for k in range(SIDE)])
    sum_y2 = Exchange(here, col_y, small_send, small_recv, 5, "y")
    sum_y2.start()
    right.finish()
    left.finish()
    sum_y2.wait()
    col_out[mine, :] = log_tgt[mine, :] - LN2 * merged([col_y[k] for k in range(SIDE)])
    sent = pl.ds(pl.multiple_of(here.c * some, 8), rest)
    taken = pl.ds(pl.multiple_of((1 - here.c) * some, 8), rest)
    col_share = to_sibling(here, col_out.at[sent], col_out.at[sent], sib_send, sib_recv, 3)
    col_share.start()
    to_sibling(here, col_out.at[taken], col_out.at[taken], sib_send, sib_recv, 3).wait_recv()

    for exchange in (sum_x, sum_y, sum_z, rows_x, sum_z2, sum_y2):
        exchange.finish()
    for copy in (core_swap, half_swap, col_swap, col_share):
        copy.wait_send()


def plan_kernel(source_count, score, row_shift, row_in, col_in, plan, row_out, col_out, buffer, done):
    pieces = done.shape[0] - 2
    width = buffer.shape[1] // pieces
    copies = [
        pltpu.make_async_copy(row_in, row_out, done.at[pieces]),
        pltpu.make_async_copy(col_in, col_out, done.at[pieces + 1]),
    ]
    for copy in copies:
        copy.start()
    for i in range(pieces):
        for q in range(i * width // LANES, (i + 1) * width // LANES):
            at = pl.ds(q * LANES, LANES)
            shift = col_in[pl.ds(q, 1), :] * LOG2E + math.log2(source_count)
            buffer[:, at] = jnp.exp2(score[:, at] + row_shift[...] + shift)
        at = pl.ds(i * width, width)
        copies.append(pltpu.make_async_copy(buffer.at[:, at], plan.at[:, at], done.at[i]))
        copies[-1].start()
    for copy in copies:
        copy.wait()


def per_device(
    coupling,
    src_left,
    emitter_distance_rightside,
    destination_distance_leftside,
    tgt_right,
    log_src,
    logarithm_destination_masses,
    tgt_potential,
):
    rows, columns = coupling.shape
    rank = src_left.shape[1]
    col_rows = columns // LANES
    some = -(-col_rows // 16) * 8
    source_count = rows * lax.axis_size("row")
    blocks = (SIDE, SIDE, 2, SHARE, columns)
    vmem = pl.BlockSpec(memory_space=pltpu.VMEM)
    anywhere = pl.BlockSpec(memory_space=pl.ANY)
    inputs = [
        coupling,
        tgt_right,
        destination_distance_leftside,
        src_left,
        emitter_distance_rightside,
        log_src.reshape(1, rows),
        logarithm_destination_masses.reshape(col_rows, LANES),
        tgt_potential.reshape(col_rows, LANES),
    ]
    outputs = pl.pallas_call(
        main_kernel,
        name="main",
        out_shape=[
            pltpu.VMEM((rows, columns), F32),
            pltpu.VMEM((rows, LANES), F32),
            pltpu.VMEM((1, rows), F32),
            pltpu.VMEM((col_rows, LANES), F32),
        ],
        in_specs=[anywhere] * len(inputs),
        out_specs=[vmem] * 4,
        scratch_shapes=[
            pltpu.VMEM(blocks, BF16),
            pltpu.VMEM(blocks, BF16),
            pltpu.VMEM((2 * rank, columns), BF16),
            pltpu.VMEM((rank, rank), F32),
            pltpu.VMEM((rank // 2, rank), F32),
            pltpu.VMEM((SIDE, rank // 2, rank), F32),
            pltpu.VMEM((SIDE, rank // 2, rank), F32),
            pltpu.VMEM((SIDE, rank // 2, rank), F32),
            pltpu.VMEM((2, rank // 2, rank), BF16),
            pltpu.VMEM((rows, LANES), F32),
            pltpu.VMEM((rows, LANES), F32),
            pltpu.VMEM((SIDE, 8, LANES), F32),
            pltpu.VMEM((col_rows, LANES), F32),
            pltpu.VMEM((some, LANES), F32),
            pltpu.VMEM((SIDE, some, LANES), F32),
            pltpu.VMEM((SIDE, some, LANES), F32),
            pltpu.VMEM((2 * rank, rank), F32),
            pltpu.VMEM((rows, rank), BF16),
            pltpu.VMEM((rows, rank), BF16),
            pltpu.VMEM((1, rows), F32),
            pltpu.VMEM((col_rows, LANES), F32),
            pltpu.VMEM((col_rows, LANES), F32),
            pltpu.SemaphoreType.DMA((len(inputs),)),
            pltpu.SemaphoreType.DMA((Gather.SENDS,)),
            pltpu.SemaphoreType.DMA((Gather.RECEIVES,)),
            pltpu.SemaphoreType.DMA((Gather.SENDS,)),
            pltpu.SemaphoreType.DMA((Gather.RECEIVES,)),
            pltpu.SemaphoreType.DMA((6,)),
            pltpu.SemaphoreType.DMA((6,)),
            pltpu.SemaphoreType.DMA((4,)),
            pltpu.SemaphoreType.DMA((4,)),
        ],
        compiler_params=pltpu.CompilerParams(
            collective_id=0, has_side_effects=True, vmem_limit_bytes=44 * 1024 * 1024
        ),
    )(*[pltpu.with_memory_space_constraint(array, pltpu.HBM) for array in inputs])
    outputs = [pltpu.with_memory_space_constraint(array, pltpu.VMEM) for array in outputs]
    pieces = columns // step_of(columns, 768)
    plan, row_potential, col_potential = pl.pallas_call(
        functools.partial(plan_kernel, source_count),
        name="plan",
        out_shape=[
            jax.ShapeDtypeStruct((rows, columns), F32),
            jax.ShapeDtypeStruct((1, rows), F32),
            jax.ShapeDtypeStruct((col_rows, LANES), F32),
        ],
        in_specs=[vmem] * 4,
        out_specs=[anywhere] * 3,
        scratch_shapes=[pltpu.VMEM((rows, columns), F32), pltpu.SemaphoreType.DMA((pieces + 2,))],
        compiler_params=pltpu.CompilerParams(vmem_limit_bytes=32 * 1024 * 1024),
    )(*outputs)
    return plan, row_potential.reshape(rows), col_potential.reshape(columns)


def solution(mesh):
    return jax.shard_map(
        per_device,
        mesh=mesh,
        in_specs=(
            P("row", "col"),
            P("row", None),
            P("row", None),
            P("row", "col"),
            P("row", "col"),
            P("row"),
            P("col"),
            P("col"),
        ),
        out_specs=(P("row", "col"), P("row"), P("col")),
        check_vma=False,
    )
```

```python
import functools
import math

import jax
import jax.numpy as jnp
from jax import lax
from jax.experimental import pallas as pl
from jax.experimental.pallas import tpu as pltpu
from jax.sharding import PartitionSpec as P

MESH = pl.DeviceIdType.MESH
BF16 = jnp.bfloat16
F32 = jnp.float32
SIDE = 4
SHARE = 4
LANES = 128
REGULARIZATION = 4.0
LOG2E = math.log2(math.e)
LN2 = math.log(2.0)
SCORE = 2.0 / REGULARIZATION * LOG2E


def wrap(v):
    return lax.rem(v + 2 * SIDE, SIDE)


class Place:
    def __init__(self):
        row = lax.axis_index("row")
        self.x = lax.axis_index("col")
        self.y = lax.div(row, 2 * SIDE)
        self.z = lax.rem(lax.div(row, 2), SIDE)
        self.c = lax.rem(row, 2)
        self.near = {axis: {step: wrap(getattr(self, axis) + step) for step in (-1, 0, 1, 2)} for axis in "xyz"}
        self.ids = {}

    def other(self, dx=0, dy=0, dz=0, dc=0):
        key = (dx, dy, dz, dc)
        if key not in self.ids:
            core = 1 - self.c if dc else self.c
            row = (self.near["y"][dy] * SIDE + self.near["z"][dz]) * 2 + core
            self.ids[key] = {"row": row, "col": self.near["x"][dx]}
        return self.ids[key]


class Gather:
    KINDS = ("A", "B")
    RECEIVES = 41
    SENDS = 3

    def __init__(self, here, raw, send, recv):
        self.here, self.raw, self.send, self.recv = here, raw, send, recv
        columns = raw.shape[-1]
        self.half, self.quarter = columns // 2, columns // 4

    def ref(self, kind, a, b, part, core=None):
        h = self.here
        core = h.c if core is None else core
        start = 0 if kind == "A" else self.half
        if part is None:
            columns = pl.ds(start, self.half)
        else:
            columns = pl.ds(start + part * self.quarter, self.quarter)
        dy, dz = (a, b) if kind == "A" else (b, a)
        y = slice(None) if dy is None else h.near["y"][dy]
        z = slice(None) if dz is None else h.near["z"][dz]
        return self.raw.at[y, z, core, :, columns]


    def copy(self, send, receive, ref, device):
        return pltpu.make_async_remote_copy(
            src_ref=ref,
            dst_ref=ref,
            send_sem=self.send.at[send],
            recv_sem=self.recv.at[receive],
            device_id=device,
            device_id_type=MESH,
        )

    def start(self, send, receive, ref, device):
        self.copy(send, receive, ref, device).start()

    def wait(self, receive, ref):
        self.copy(0, receive, ref, self.here.other(dc=1)).wait_recv()

    def along(self, kind, first, step):
        if first == (kind == "A"):
            return self.here.other(dz=step)
        return self.here.other(dy=step)


    @staticmethod
    def side(step):
        return 0 if step == 1 else 1

    def number(self, kind, number):
        return number + (0 if kind == "A" else 20)

    def first_number(self, kind, part, step):
        return self.number(kind, part * 2 + self.side(step))

    def last_number(self, kind, b, part, step):
        ends = part != self.side(step)
        return self.number(kind, 14 + self.side(step) if ends else 8 + 2 * b + part)

    def first(self, kind, part, step):
        number = self.first_number(kind, part, step)
        self.start(0, number, self.ref(kind, 0, 0, part), self.along(kind, True, step))

    def wait_first(self, kind, part, step):
        self.wait(self.first_number(kind, part, step), self.ref(kind, 0, -step, part))

    def first_on(self, kind, step):
        part = self.side(step)
        self.start(0, self.number(kind, 4 + part), self.ref(kind, 0, -step, part), self.along(kind, True, step))

    def wait_first_on(self, kind, step):
        part = self.side(step)
        self.wait(self.number(kind, 4 + part), self.ref(kind, 0, 2, part))

    def last(self, kind, b, part, step):
        number = self.last_number(kind, b, part, step)
        self.start(1, number, self.ref(kind, 0, b, part), self.along(kind, False, step))

    def wait_last(self, kind, b, step):
        part = self.side(step)
        self.wait(self.last_number(kind, b, part, step), self.ref(kind, -step, b, part))

    def wait_ending(self, kind, step):
        part = 1 - self.side(step)
        self.wait(self.last_number(kind, 0, part, step), self.ref(kind, -step, None, part))

    def last_on(self, kind, b, step):
        part = self.side(step)
        self.start(1, self.number(kind, 17 + b), self.ref(kind, -step, b, part), self.along(kind, False, step))

    def wait_last_on(self, kind, b):
        self.wait(self.number(kind, 17 + b), self.ref(kind, 2, b, None))

    def to_sibling(self, kind, a, b, part=None):
        self.start(2, 40, self.ref(kind, a, b, part), self.here.other(dc=1))

    STEPS = ((1, 0), (-1, 1))

    def step(self, number):
        getattr(self, "step_%d" % number)()

    def step_0(self):
        for kind in self.KINDS:
            for step, part in self.STEPS:
                self.first(kind, part, step)
        for kind in self.KINDS:
            for step, part in self.STEPS:
                self.first(kind, 1 - part, step)
        for kind in self.KINDS:
            for step, part in self.STEPS:
                self.last(kind, 0, part, step)
        for kind in self.KINDS:
            for step, part in self.STEPS:
                self.last(kind, 0, 1 - part, step)

    def step_1(self):
        for kind in self.KINDS:
            for step, part in self.STEPS:
                self.wait_first(kind, part, step)
                self.first_on(kind, step)
                self.last(kind, -step, part, step)

    def step_2(self):
        for kind in self.KINDS:
            for step, part in self.STEPS:
                self.wait_first(kind, 1 - part, step)
                self.last(kind, -step, 1 - part, -step)

    def step_3(self):
        for kind in self.KINDS:
            for step, part in self.STEPS:
                self.wait_last(kind, 0, step)
                self.last_on(kind, 0, step)
        for kind in self.KINDS:
            for b in (-1, 1):
                for step, part in self.STEPS:
                    self.last(kind, b, 1 - part, step)

    def step_4(self):
        for kind in self.KINDS:
            for step, part in self.STEPS:
                self.wait_first_on(kind, step)
                self.last(kind, 2, part, step)
        for kind in self.KINDS:
            self.to_sibling(kind, 0, None)

    def step_5(self):
        for kind in self.KINDS:
            for b in (-1, 1):
                for step, part in self.STEPS:
                    self.wait_last(kind, b, step)
                    self.last_on(kind, b, step)
        for kind in self.KINDS:
            for step, part in self.STEPS:
                self.last(kind, 2, 1 - part, step)

    def step_6(self):
        for kind in self.KINDS:
            for step, part in self.STEPS:
                self.wait_last(kind, 2, step)
                self.last_on(kind, 2, step)
        for kind in self.KINDS:
            for step, part in self.STEPS:
                self.to_sibling(kind, -step, None, part)

    def step_7(self):
        for kind in self.KINDS:
            for step, part in self.STEPS:
                self.wait_ending(kind, step)
                self.to_sibling(kind, -step, None, 1 - part)

    def step_8(self):
        for b in (0, -1, 1, 2):
            for kind in self.KINDS:
                self.wait_last_on(kind, b)
                self.to_sibling(kind, 2, b)

    def step_9(self):
        self.wait(40, self.raw.at[:, :, 1 - self.here.c])

    def finish(self):
        for send, ref in enumerate((self.raw.at[0, 0:3, 0], self.raw.at[0:3, :, 0], self.raw.at[:, :, 0])):
            self.copy(send, 0, ref, self.here.other(dc=1)).wait_send()


class Exchange:
    def __init__(self, here, buffer, send, recv, number, axis):
        self.here, self.buffer, self.axis = here, buffer, axis
        self.send, self.recv = send.at[number], recv.at[number]

    def copy(self, ref, device):
        return pltpu.make_async_remote_copy(
            src_ref=ref,
            dst_ref=ref,
            send_sem=self.send,
            recv_sem=self.recv,
            device_id=device,
            device_id_type=MESH,
        )

    def start(self):
        for step in (2, 1, -1):
            own = self.buffer.at[getattr(self.here, self.axis)]
            self.copy(own, self.here.other(**{"d" + self.axis: step})).start()

    def wait(self):
        self.copy(self.buffer.at[0:3], self.here.other(dc=1)).wait_recv()

    def finish(self):
        self.copy(self.buffer.at[0:3], self.here.other(dc=1)).wait_send()


def to_sibling(here, src, dst, send, recv, index):
    return pltpu.make_async_remote_copy(
        src_ref=src,
        dst_ref=dst,
        send_sem=send.at[index],
        recv_sem=recv.at[index],
        device_id=here.other(dc=1),
        device_id_type=MESH,
    )


def added(parts):
    return (parts[0] + parts[1]) + (parts[2] + parts[3])


def merged(parts):
    peak = functools.reduce(jnp.maximum, parts)
    total = functools.reduce(jnp.add, [jnp.exp2(part - peak) for part in parts])
    return peak + jnp.log2(total)


def step_of(columns, most):
    return max(s for s in range(LANES, most + 1, LANES) if columns % s == 0)


def main_kernel(
    coupling_hbm, tgt_right_hbm, tgt_left_hbm,
    src_left_hbm, src_right_hbm, log_src_hbm, log_tgt_hbm, tgt_potential_hbm,
    wide, row_shift_out, row_out, col_out,
    raw_right, raw_left, image, core_part, core_sib, core_sums, core_half,
    peaks, totals, row_parts, col_all, col_sib, col_sums,
    src_left, src_right, log_src, log_tgt, tgt_potential,
    local, right_send, right_recv, left_send, left_recv,
    small_send, small_recv, sib_send, sib_recv,
):
    here = Place()
    columns = wide.shape[1]
    rows = wide.shape[0]

    loads = []
    for k, (source, target) in enumerate((
        (tgt_right_hbm, raw_right.at[here.y, here.z, here.c]),
        (src_right_hbm, src_right),
        (tgt_left_hbm, raw_left.at[here.y, here.z, here.c]),
        (coupling_hbm, wide),
        (src_left_hbm, src_left),
        (log_src_hbm, log_src),
        (log_tgt_hbm, log_tgt),
        (tgt_potential_hbm, tgt_potential),
    )):
        loads.append(pltpu.make_async_copy(source, target, local.at[k]))
        loads[-1].start()

    barrier = pltpu.get_barrier_semaphore()
    partners = [here.other(dc=1)]
    for axis in "xyz":
        partners += [here.other(**{"d" + axis: step}) for step in (1, -1, 2)]
    for partner in partners:
        pl.semaphore_signal(barrier, inc=1, device_id=partner, device_id_type=MESH)
    loads[0].wait()
    pl.semaphore_wait(barrier, len(partners))

    right = Gather(here, raw_right, right_send, right_recv)
    left = Gather(here, raw_left, left_send, left_recv)
    right.step(0)

    for k in (1, 2, 3):
        loads[k].wait()
    side = src_right[...].astype(F32).T.astype(BF16)
    side = jnp.concatenate([side, side], axis=1)
    width = step_of(columns, 3072)

    def image_step(i, _):
        at = pl.ds(pl.multiple_of(i * width, width), width)
        entries = wide[:, at]
        high = entries.astype(BF16)
        low = (entries - high.astype(F32)).astype(BF16)
        value = jnp.dot(side, jnp.concatenate([high, low], axis=0), preferred_element_type=F32)
        value_high = value.astype(BF16)
        image[0:LANES, at] = value_high
        image[LANES : 2 * LANES, at] = (value - value_high.astype(F32)).astype(BF16)
        return 0

    steps = columns // width
    cuts = [0] + [(steps * (k + 2)) // 5 for k in range(3)] + [steps]
    for k in range(4):
        lax.fori_loop(cuts[k], cuts[k + 1], image_step, 0)
        right.step(k + 1)
    right.step(5)
    left.step(0)
    right.step(6)
    right.step(7)
    right.step(8)
    left.step(1)
    left.step(2)
    right.step(9)

    factor = raw_right[...].reshape(LANES, columns)
    parts = lax.dot_general(image[...], factor, (((1,), (1,)), ((), ())), preferred_element_type=F32)
    core_part[...] = parts[0:LANES] + parts[LANES : 2 * LANES]

    part_rows = LANES // 2
    mine = pl.ds(pl.multiple_of(here.c * part_rows, part_rows), part_rows)
    theirs = pl.ds(pl.multiple_of((1 - here.c) * part_rows, part_rows), part_rows)
    core_swap = to_sibling(here, core_part.at[theirs], core_sib, sib_send, sib_recv, 0)
    core_swap.start()
    left.step(3)
    core_swap.wait_recv()
    total = core_part[mine] + core_sib[...]
    piece = part_rows // 2
    totals_of = [total[0:piece], total[piece:]]
    sums = []

    def sum_start(stage):
        for p, order in enumerate(("xyz", "yzx")):
            number = 2 * stage + p
            core_sums[number, getattr(here, order[stage])] = totals_of[p]
            sums.append(Exchange(here, core_sums.at[number], small_send, small_recv, number, order[stage]))
            sums[-1].start()

    def sum_wait(stage):
        for p in range(2):
            number = 2 * stage + p
            sums[number].wait()
            totals_of[p] = added([core_sums[number, k] for k in range(SIDE)])

    sum_start(0)
    left.step(4)
    left.step(5)
    sum_wait(0)
    sum_start(1)
    left.step(6)
    left.step(7)
    sum_wait(1)
    sum_start(2)
    left.step(8)
    sum_wait(2)
    core_half[here.c] = jnp.concatenate(totals_of, axis=0).astype(BF16)
    half_swap = to_sibling(here, core_half.at[here.c], core_half.at[here.c], sib_send, sib_recv, 1)
    half_swap.start()
    for k in range(4, 8):
        loads[k].wait()
    left.step(9)
    to_sibling(here, core_half.at[1 - here.c], core_half.at[1 - here.c], sib_send, sib_recv, 1).wait_recv()
    core = core_half[...].reshape(LANES, LANES)
    rows_cost = jnp.dot(src_left[...], core, preferred_element_type=F32).astype(BF16)

    span = step_of(columns, 5120)

    peaks[...] = jnp.full_like(peaks, -jnp.inf)
    tiles = span // LANES

    def score_step(i, _):
        at = pl.ds(pl.multiple_of(i * span, span), span)
        factor = raw_left[:, :, :, :, at].reshape(LANES, span)
        score = jnp.dot(rows_cost, factor, preferred_element_type=F32) * SCORE
        wide[:, at] = score
        peak = peaks[...]
        for q in range(tiles):
            shift = tgt_potential[pl.ds(i * tiles + q, 1), :] * LOG2E
            peak = jnp.maximum(peak, score[:, q * LANES : (q + 1) * LANES] + shift)
        peaks[...] = peak
        return 0

    lax.fori_loop(0, columns // span, score_step, 0)

    totals[...] = jnp.zeros_like(totals)
    reach = step_of(columns, 3072)
    pieces = reach // LANES

    def total_step(i, _):
        peak = peaks[...]
        total = totals[...]
        for q in range(pieces):
            at = pl.ds(pl.multiple_of(i * reach + q * LANES, LANES), LANES)
            shift = tgt_potential[pl.ds(i * pieces + q, 1), :] * LOG2E
            total = total + jnp.exp2(wide[:, at] + shift - peak)
        totals[...] = total
        return 0

    lax.fori_loop(0, columns // reach, total_step, 0)
    lane_peak = peaks[...].T
    row_peak = jnp.max(lane_peak, axis=0, keepdims=True)
    row_total = jnp.sum(totals[...].T * jnp.exp2(lane_peak - row_peak), axis=0, keepdims=True)
    row_parts[here.x] = jnp.broadcast_to(row_peak + jnp.log2(row_total), row_parts.shape[1:])
    rows_x = Exchange(here, row_parts, small_send, small_recv, 6, "x")
    sums.append(rows_x)
    rows_x.start()
    rows_x.wait()
    row_sum = merged([row_parts[k] for k in range(SIDE)])[0:1]
    row_potential = log_src[...] - LN2 * row_sum
    row_out[...] = row_potential
    row_shift_out[...] = jnp.broadcast_to(row_potential * LOG2E, (LANES, LANES)).T

    def col_step(i, _):
        for q in range(pieces):
            at = pl.ds(pl.multiple_of(i * reach + q * LANES, LANES), LANES)
            score = (wide[:, at] + row_shift_out[...]).reshape(rows // 8, 8, LANES)
            peak = jnp.max(score, axis=0)
            total = jnp.sum(jnp.exp2(score - peak[None]), axis=0)
            top = jnp.max(peak, axis=0, keepdims=True)
            total = jnp.sum(total * jnp.exp2(peak - top), axis=0, keepdims=True)
            col_all[pl.ds(i * pieces + q, 1), :] = top + jnp.log2(total)
        return 0

    lax.fori_loop(0, columns // reach, col_step, 0)

    col_rows = col_all.shape[0]
    some = col_sib.shape[0]
    rest = col_rows - some
    mine = pl.ds(pl.multiple_of(here.c * rest, 8), some)
    theirs = pl.ds(pl.multiple_of((1 - here.c) * rest, 8), some)
    col_swap = to_sibling(here, col_all.at[theirs], col_sib, sib_send, sib_recv, 2)
    col_swap.start()
    col_swap.wait_recv()
    total = merged([col_all[mine, :], col_sib[...]])
    piece = some // 2
    totals_of[:] = [total[0:piece], total[piece:]]

    def col_start(stage):
        for p, order in enumerate(("zy", "yz")):
            number = 2 * stage + p
            col_sums[number, getattr(here, order[stage])] = totals_of[p]
            sums.append(Exchange(here, col_sums.at[number], small_send, small_recv, 7 + number, order[stage]))
            sums[-1].start()

    def col_wait(stage):
        for p in range(2):
            number = 2 * stage + p
            sums[7 + number].wait()
            totals_of[p] = merged([col_sums[number, k] for k in range(SIDE)])

    col_start(0)
    col_wait(0)
    col_start(1)
    right.finish()
    left.finish()
    col_wait(1)
    col_out[mine, :] = log_tgt[mine, :] - LN2 * jnp.concatenate(totals_of, axis=0)
    sent = pl.ds(pl.multiple_of(here.c * some, 8), rest)
    taken = pl.ds(pl.multiple_of((1 - here.c) * some, 8), rest)
    col_share = to_sibling(here, col_out.at[sent], col_out.at[sent], sib_send, sib_recv, 3)
    col_share.start()
    to_sibling(here, col_out.at[taken], col_out.at[taken], sib_send, sib_recv, 3).wait_recv()

    for exchange in sums:
        exchange.finish()
    for copy in (core_swap, half_swap, col_swap, col_share):
        copy.wait_send()


def plan_kernel(source_count, score, row_shift, row_in, col_in, plan, row_out, col_out, buffer, done):
    pieces = done.shape[0] - 2
    width = buffer.shape[1] // pieces
    copies = [
        pltpu.make_async_copy(row_in, row_out, done.at[pieces]),
        pltpu.make_async_copy(col_in, col_out, done.at[pieces + 1]),
    ]
    for copy in copies:
        copy.start()
    for i in range(pieces):
        for q in range(i * width // LANES, (i + 1) * width // LANES):
            at = pl.ds(q * LANES, LANES)
            shift = col_in[pl.ds(q, 1), :] * LOG2E + math.log2(source_count)
            buffer[:, at] = jnp.exp2(score[:, at] + row_shift[...] + shift)
        at = pl.ds(i * width, width)
        copies.append(pltpu.make_async_copy(buffer.at[:, at], plan.at[:, at], done.at[i]))
        copies[-1].start()
    for copy in copies:
        copy.wait()


def per_device(
    coupling,
    src_left,
    emitter_distance_rightside,
    destination_distance_leftside,
    tgt_right,
    log_src,
    logarithm_destination_masses,
    tgt_potential,
):
    rows, columns = coupling.shape
    rank = src_left.shape[1]
    col_rows = columns // LANES
    some = -(-col_rows // 32) * 16
    source_count = rows * lax.axis_size("row")
    blocks = (SIDE, SIDE, 2, SHARE, columns)
    vmem = pl.BlockSpec(memory_space=pltpu.VMEM)
    anywhere = pl.BlockSpec(memory_space=pl.ANY)
    inputs = [
        coupling,
        tgt_right,
        destination_distance_leftside,
        src_left,
        emitter_distance_rightside,
        log_src.reshape(1, rows),
        logarithm_destination_masses.reshape(col_rows, LANES),
        tgt_potential.reshape(col_rows, LANES),
    ]
    outputs = pl.pallas_call(
        main_kernel,
        name="main",
        out_shape=[
            pltpu.VMEM((rows, columns), F32),
            pltpu.VMEM((rows, LANES), F32),
            pltpu.VMEM((1, rows), F32),
            pltpu.VMEM((col_rows, LANES), F32),
        ],
        in_specs=[anywhere] * len(inputs),
        out_specs=[vmem] * 4,
        scratch_shapes=[
            pltpu.VMEM(blocks, BF16),
            pltpu.VMEM(blocks, BF16),
            pltpu.VMEM((2 * rank, columns), BF16),
            pltpu.VMEM((rank, rank), F32),
            pltpu.VMEM((rank // 2, rank), F32),
            pltpu.VMEM((6, SIDE, rank // 4, rank), F32),
            pltpu.VMEM((2, rank // 2, rank), BF16),
            pltpu.VMEM((rows, LANES), F32),
            pltpu.VMEM((rows, LANES), F32),
            pltpu.VMEM((SIDE, 8, LANES), F32),
            pltpu.VMEM((col_rows, LANES), F32),
            pltpu.VMEM((some, LANES), F32),
            pltpu.VMEM((4, SIDE, some // 2, LANES), F32),
            pltpu.VMEM((rows, rank), BF16),
            pltpu.VMEM((rows, rank), BF16),
            pltpu.VMEM((1, rows), F32),
            pltpu.VMEM((col_rows, LANES), F32),
            pltpu.VMEM((col_rows, LANES), F32),
            pltpu.SemaphoreType.DMA((len(inputs),)),
            pltpu.SemaphoreType.DMA((Gather.SENDS,)),
            pltpu.SemaphoreType.DMA((Gather.RECEIVES,)),
            pltpu.SemaphoreType.DMA((Gather.SENDS,)),
            pltpu.SemaphoreType.DMA((Gather.RECEIVES,)),
            pltpu.SemaphoreType.DMA((11,)),
            pltpu.SemaphoreType.DMA((11,)),
            pltpu.SemaphoreType.DMA((4,)),
            pltpu.SemaphoreType.DMA((4,)),
        ],
        compiler_params=pltpu.CompilerParams(
            collective_id=0, has_side_effects=True, vmem_limit_bytes=44 * 1024 * 1024
        ),
    )(*[pltpu.with_memory_space_constraint(array, pltpu.HBM) for array in inputs])
    outputs = [pltpu.with_memory_space_constraint(array, pltpu.VMEM) for array in outputs]
    pieces = columns // step_of(columns, 768)
    plan, row_potential, col_potential = pl.pallas_call(
        functools.partial(plan_kernel, source_count),
        name="plan",
        out_shape=[
            jax.ShapeDtypeStruct((rows, columns), F32),
            jax.ShapeDtypeStruct((1, rows), F32),
            jax.ShapeDtypeStruct((col_rows, LANES), F32),
        ],
        in_specs=[vmem] * 4,
        out_specs=[anywhere] * 3,
        scratch_shapes=[pltpu.VMEM((rows, columns), F32), pltpu.SemaphoreType.DMA((pieces + 2,))],
        compiler_params=pltpu.CompilerParams(vmem_limit_bytes=32 * 1024 * 1024),
    )(*outputs)
    return plan, row_potential.reshape(rows), col_potential.reshape(columns)


def solution(mesh):
    return jax.shard_map(
        per_device,
        mesh=mesh,
        in_specs=(
            P("row", "col"),
            P("row", None),
            P("row", None),
            P("row", "col"),
            P("row", "col"),
            P("row"),
            P("col"),
            P("col"),
        ),
        out_specs=(P("row", "col"), P("row"), P("col")),
        check_vma=False,
    )
```

```python
import functools
import math

import jax
import jax.numpy as jnp
from jax import lax
from jax.experimental import pallas as pl
from jax.experimental.pallas import tpu as pltpu
from jax.sharding import PartitionSpec as P

MESH = pl.DeviceIdType.MESH
BF16 = jnp.bfloat16
F32 = jnp.float32
SIDE = 4
SHARE = 4
LANES = 128
REGULARIZATION = 4.0
LOG2E = math.log2(math.e)
LN2 = math.log(2.0)
SCORE = 2.0 / REGULARIZATION * LOG2E


def wrap(v):
    return lax.rem(v + 2 * SIDE, SIDE)


class Place:
    def __init__(self):
        row = lax.axis_index("row")
        self.x = lax.axis_index("col")
        self.y = lax.div(row, 2 * SIDE)
        self.z = lax.rem(lax.div(row, 2), SIDE)
        self.c = lax.rem(row, 2)
        self.near = {axis: {step: wrap(getattr(self, axis) + step) for step in (-1, 0, 1, 2)} for axis in "xyz"}
        self.ids = {}

    def other(self, dx=0, dy=0, dz=0, dc=0):
        key = (dx, dy, dz, dc)
        if key not in self.ids:
            core = 1 - self.c if dc else self.c
            row = (self.near["y"][dy] * SIDE + self.near["z"][dz]) * 2 + core
            self.ids[key] = {"row": row, "col": self.near["x"][dx]}
        return self.ids[key]


class Gather:
    KINDS = ("A", "B")
    RECEIVES = 41
    SENDS = 3

    def __init__(self, here, raw, send, recv):
        self.here, self.raw, self.send, self.recv = here, raw, send, recv
        columns = raw.shape[-1]
        self.half, self.quarter = columns // 2, columns // 4

    def ref(self, kind, a, b, part, core=None):
        h = self.here
        core = h.c if core is None else core
        start = 0 if kind == "A" else self.half
        if part is None:
            columns = pl.ds(start, self.half)
        else:
            columns = pl.ds(start + part * self.quarter, self.quarter)
        dy, dz = (a, b) if kind == "A" else (b, a)
        y = slice(None) if dy is None else h.near["y"][dy]
        z = slice(None) if dz is None else h.near["z"][dz]
        return self.raw.at[y, z, core, :, columns]


    def copy(self, send, receive, ref, device):
        return pltpu.make_async_remote_copy(
            src_ref=ref,
            dst_ref=ref,
            send_sem=self.send.at[send],
            recv_sem=self.recv.at[receive],
            device_id=device,
            device_id_type=MESH,
        )

    def start(self, send, receive, ref, device):
        self.copy(send, receive, ref, device).start()

    def wait(self, receive, ref):
        self.copy(0, receive, ref, self.here.other(dc=1)).wait_recv()

    def along(self, kind, first, step):
        if first == (kind == "A"):
            return self.here.other(dz=step)
        return self.here.other(dy=step)


    @staticmethod
    def side(step):
        return 0 if step == 1 else 1

    def number(self, kind, number):
        return number + (0 if kind == "A" else 20)

    def first_number(self, kind, part, step):
        return self.number(kind, part * 2 + self.side(step))

    def last_number(self, kind, b, part, step):
        ends = part != self.side(step)
        return self.number(kind, 14 + self.side(step) if ends else 8 + 2 * b + part)

    def first(self, kind, part, step):
        number = self.first_number(kind, part, step)
        self.start(0, number, self.ref(kind, 0, 0, part), self.along(kind, True, step))

    def wait_first(self, kind, part, step):
        self.wait(self.first_number(kind, part, step), self.ref(kind, 0, -step, part))

    def first_on(self, kind, step):
        part = self.side(step)
        self.start(0, self.number(kind, 4 + part), self.ref(kind, 0, -step, part), self.along(kind, True, step))

    def wait_first_on(self, kind, step):
        part = self.side(step)
        self.wait(self.number(kind, 4 + part), self.ref(kind, 0, 2, part))

    def last(self, kind, b, part, step):
        number = self.last_number(kind, b, part, step)
        self.start(1, number, self.ref(kind, 0, b, part), self.along(kind, False, step))

    def wait_last(self, kind, b, step):
        part = self.side(step)
        self.wait(self.last_number(kind, b, part, step), self.ref(kind, -step, b, part))

    def wait_ending(self, kind, step):
        part = 1 - self.side(step)
        self.wait(self.last_number(kind, 0, part, step), self.ref(kind, -step, None, part))

    def last_on(self, kind, b, step):
        part = self.side(step)
        self.start(1, self.number(kind, 17 + b), self.ref(kind, -step, b, part), self.along(kind, False, step))

    def wait_last_on(self, kind, b):
        self.wait(self.number(kind, 17 + b), self.ref(kind, 2, b, None))

    def to_sibling(self, kind, a, b, part=None):
        self.start(2, 40, self.ref(kind, a, b, part), self.here.other(dc=1))

    STEPS = ((1, 0), (-1, 1))

    def step(self, number):
        getattr(self, "step_%d" % number)()

    def step_0(self):
        for kind in self.KINDS:
            for step, part in self.STEPS:
                self.first(kind, part, step)
        for kind in self.KINDS:
            for step, part in self.STEPS:
                self.first(kind, 1 - part, step)
        for kind in self.KINDS:
            for step, part in self.STEPS:
                self.last(kind, 0, part, step)
        for kind in self.KINDS:
            for step, part in self.STEPS:
                self.last(kind, 0, 1 - part, step)

    def step_1(self):
        for kind in self.KINDS:
            for step, part in self.STEPS:
                self.wait_first(kind, part, step)
                self.first_on(kind, step)
                self.last(kind, -step, part, step)

    def step_2(self):
        for kind in self.KINDS:
            for step, part in self.STEPS:
                self.wait_first(kind, 1 - part, step)
                self.last(kind, -step, 1 - part, -step)

    def step_3(self):
        for kind in self.KINDS:
            for step, part in self.STEPS:
                self.wait_last(kind, 0, step)
                self.last_on(kind, 0, step)
        for kind in self.KINDS:
            for b in (-1, 1):
                for step, part in self.STEPS:
                    self.last(kind, b, 1 - part, step)

    def step_4(self):
        for kind in self.KINDS:
            for step, part in self.STEPS:
                self.wait_first_on(kind, step)
                self.last(kind, 2, part, step)
        for kind in self.KINDS:
            self.to_sibling(kind, 0, None)

    def step_5(self):
        for kind in self.KINDS:
            for b in (-1, 1):
                for step, part in self.STEPS:
                    self.wait_last(kind, b, step)
                    self.last_on(kind, b, step)
        for kind in self.KINDS:
            for step, part in self.STEPS:
                self.last(kind, 2, 1 - part, step)

    def step_6(self):
        for kind in self.KINDS:
            for step, part in self.STEPS:
                self.wait_last(kind, 2, step)
                self.last_on(kind, 2, step)
        for kind in self.KINDS:
            for step, part in self.STEPS:
                self.to_sibling(kind, -step, None, part)

    def step_7(self):
        for kind in self.KINDS:
            for step, part in self.STEPS:
                self.wait_ending(kind, step)
                self.to_sibling(kind, -step, None, 1 - part)

    def step_8(self):
        for b in (0, -1, 1, 2):
            for kind in self.KINDS:
                self.wait_last_on(kind, b)
                self.to_sibling(kind, 2, b)

    def step_9(self):
        self.wait(40, self.raw.at[:, :, 1 - self.here.c])

    def finish(self):
        for send, ref in enumerate((self.raw.at[0, 0:3, 0], self.raw.at[0:3, :, 0], self.raw.at[:, :, 0])):
            self.copy(send, 0, ref, self.here.other(dc=1)).wait_send()


class Exchange:
    def __init__(self, here, buffer, send, recv, number, axis):
        self.here, self.buffer, self.axis = here, buffer, axis
        self.send, self.recv = send.at[number], recv.at[number]

    def copy(self, ref, device):
        return pltpu.make_async_remote_copy(
            src_ref=ref,
            dst_ref=ref,
            send_sem=self.send,
            recv_sem=self.recv,
            device_id=device,
            device_id_type=MESH,
        )

    def start(self):
        for step in (2, 1, -1):
            own = self.buffer.at[getattr(self.here, self.axis)]
            self.copy(own, self.here.other(**{"d" + self.axis: step})).start()

    def wait(self):
        self.copy(self.buffer.at[0:3], self.here.other(dc=1)).wait_recv()

    def finish(self):
        self.copy(self.buffer.at[0:3], self.here.other(dc=1)).wait_send()


def to_sibling(here, src, dst, send, recv, index):
    return pltpu.make_async_remote_copy(
        src_ref=src,
        dst_ref=dst,
        send_sem=send.at[index],
        recv_sem=recv.at[index],
        device_id=here.other(dc=1),
        device_id_type=MESH,
    )


def added(parts):
    return (parts[0] + parts[1]) + (parts[2] + parts[3])


def merged(parts):
    peak = functools.reduce(jnp.maximum, parts)
    total = functools.reduce(jnp.add, [jnp.exp2(part - peak) for part in parts])
    return peak + jnp.log2(total)


def step_of(columns, most):
    return max(s for s in range(LANES, most + 1, LANES) if columns % s == 0)


def main_kernel(
    coupling_hbm, tgt_right_hbm, tgt_left_hbm,
    src_left_hbm, src_right_hbm, log_src_hbm, log_tgt_hbm, tgt_potential_hbm,
    wide, row_shift_out, row_out, col_out,
    raw_right, raw_left, image, core_part, core_sib, core_sums, core_half,
    peaks, totals, row_parts, col_all, col_sib, col_sums,
    src_left, src_right, log_src, log_tgt, tgt_potential,
    local, right_send, right_recv, left_send, left_recv,
    small_send, small_recv, sib_send, sib_recv,
):
    here = Place()
    columns = wide.shape[1]
    rows = wide.shape[0]

    barrier = pltpu.get_barrier_semaphore()
    partners = [here.other(dc=1)]
    for axis in "xyz":
        partners += [here.other(**{"d" + axis: step}) for step in (1, -1, 2)]
    for partner in partners:
        pl.semaphore_signal(barrier, inc=1, device_id=partner, device_id_type=MESH)
    loads = []
    for k, (source, target) in enumerate((
        (tgt_right_hbm, raw_right.at[here.y, here.z, here.c]),
        (src_right_hbm, src_right),
        (tgt_left_hbm, raw_left.at[here.y, here.z, here.c]),
        (coupling_hbm, wide),
        (src_left_hbm, src_left),
        (log_src_hbm, log_src),
        (log_tgt_hbm, log_tgt),
        (tgt_potential_hbm, tgt_potential),
    )):
        loads.append(pltpu.make_async_copy(source, target, local.at[k]))
        loads[-1].start()

    loads[0].wait()
    pl.semaphore_wait(barrier, len(partners))

    right = Gather(here, raw_right, right_send, right_recv)
    left = Gather(here, raw_left, left_send, left_recv)
    right.step(0)

    for k in (1, 2, 3):
        loads[k].wait()
    side = jnp.concatenate([src_right[...], src_right[...]], axis=0)
    width = step_of(columns, 3072)

    def image_step(i, _):
        at = pl.ds(pl.multiple_of(i * width, width), width)
        entries = wide[:, at]
        high = entries.astype(BF16)
        low = (entries - high.astype(F32)).astype(BF16)
        value = lax.dot_general(
            jnp.concatenate([high, low], axis=0), side, (((0,), (0,)), ((), ())), preferred_element_type=F32
        )
        value_high = value.astype(BF16)
        image[at, 0:LANES] = value_high
        image[at, LANES : 2 * LANES] = (value - value_high.astype(F32)).astype(BF16)
        return 0

    steps = columns // width
    cuts = [0, 0, (steps * 2) // 5, (steps * 3) // 5, steps]
    for k in range(4):
        lax.fori_loop(cuts[k], cuts[k + 1], image_step, 0)
        right.step(k + 1)
    right.step(5)
    left.step(0)
    right.step(6)
    right.step(7)
    right.step(8)
    left.step(1)
    left.step(2)
    right.step(9)

    factor = raw_right[...].reshape(LANES, columns)
    parts = jnp.dot(factor, image[...], preferred_element_type=F32)
    core_part[...] = parts[:, 0:LANES] + parts[:, LANES : 2 * LANES]

    part_rows = LANES // 2
    mine = pl.ds(pl.multiple_of(here.c * part_rows, part_rows), part_rows)
    theirs = pl.ds(pl.multiple_of((1 - here.c) * part_rows, part_rows), part_rows)
    core_swap = to_sibling(here, core_part.at[theirs], core_sib, sib_send, sib_recv, 0)
    core_swap.start()
    left.step(3)
    core_swap.wait_recv()
    total = core_part[mine] + core_sib[...]
    piece = part_rows // 2
    totals_of = [total[0:piece], total[piece:]]
    sums = []

    def sum_start(stage):
        for p, order in enumerate(("xyz", "yzx")):
            number = 2 * stage + p
            core_sums[number, getattr(here, order[stage])] = totals_of[p]
            sums.append(Exchange(here, core_sums.at[number], small_send, small_recv, number, order[stage]))
            sums[-1].start()

    def sum_wait(stage):
        for p in range(2):
            number = 2 * stage + p
            sums[number].wait()
            totals_of[p] = added([core_sums[number, k] for k in range(SIDE)])

    sum_start(0)
    left.step(4)
    left.step(5)
    sum_wait(0)
    sum_start(1)
    left.step(6)
    left.step(7)
    sum_wait(1)
    sum_start(2)
    left.step(8)
    sum_wait(2)
    core_half[here.c] = jnp.concatenate(totals_of, axis=0).astype(BF16)
    half_swap = to_sibling(here, core_half.at[here.c], core_half.at[here.c], sib_send, sib_recv, 1)
    half_swap.start()
    for k in range(4, 8):
        loads[k].wait()
    left.step(9)
    to_sibling(here, core_half.at[1 - here.c], core_half.at[1 - here.c], sib_send, sib_recv, 1).wait_recv()
    core = core_half[...].reshape(LANES, LANES)
    rows_cost = lax.dot_general(
        src_left[...], core, (((1,), (1,)), ((), ())), preferred_element_type=F32
    ).astype(BF16)

    span = step_of(columns, 5120)

    peaks[...] = jnp.full_like(peaks, -jnp.inf)
    tiles = span // LANES

    def score_step(i, _):
        at = pl.ds(pl.multiple_of(i * span, span), span)
        factor = raw_left[:, :, :, :, at].reshape(LANES, span)
        score = jnp.dot(rows_cost, factor, preferred_element_type=F32) * SCORE
        wide[:, at] = score
        peak = peaks[...]
        for q in range(tiles):
            shift = tgt_potential[pl.ds(i * tiles + q, 1), :] * LOG2E
            peak = jnp.maximum(peak, score[:, q * LANES : (q + 1) * LANES] + shift)
        peaks[...] = peak
        return 0

    lax.fori_loop(0, columns // span, score_step, 0)

    totals[...] = jnp.zeros_like(totals)
    reach = step_of(columns, 3072)
    pieces = reach // LANES

    def total_step(i, _):
        peak = peaks[...]
        total = totals[...]
        for q in range(pieces):
            at = pl.ds(pl.multiple_of(i * reach + q * LANES, LANES), LANES)
            shift = tgt_potential[pl.ds(i * pieces + q, 1), :] * LOG2E
            total = total + jnp.exp2(wide[:, at] + shift - peak)
        totals[...] = total
        return 0

    lax.fori_loop(0, columns // reach, total_step, 0)
    lane_peak = peaks[...].T
    row_peak = jnp.max(lane_peak, axis=0, keepdims=True)
    row_total = jnp.sum(totals[...].T * jnp.exp2(lane_peak - row_peak), axis=0, keepdims=True)
    row_parts[here.x] = jnp.broadcast_to(row_peak + jnp.log2(row_total), row_parts.shape[1:])
    rows_x = Exchange(here, row_parts, small_send, small_recv, 6, "x")
    sums.append(rows_x)
    rows_x.start()
    rows_x.wait()
    row_sum = merged([row_parts[k] for k in range(SIDE)])[0:1]
    row_potential = log_src[...] - LN2 * row_sum
    row_out[...] = row_potential
    row_shift_out[...] = jnp.broadcast_to(row_potential * LOG2E, (LANES, LANES)).T

    def col_step(i, _):
        for q in range(pieces):
            at = pl.ds(pl.multiple_of(i * reach + q * LANES, LANES), LANES)
            score = (wide[:, at] + row_shift_out[...]).reshape(rows // 8, 8, LANES)
            peak = jnp.max(score, axis=0)
            total = jnp.sum(jnp.exp2(score - peak[None]), axis=0)
            top = jnp.max(peak, axis=0, keepdims=True)
            total = jnp.sum(total * jnp.exp2(peak - top), axis=0, keepdims=True)
            col_all[pl.ds(i * pieces + q, 1), :] = top + jnp.log2(total)
        return 0

    lax.fori_loop(0, columns // reach, col_step, 0)

    col_rows = col_all.shape[0]
    some = col_sib.shape[0]
    rest = col_rows - some
    mine = pl.ds(pl.multiple_of(here.c * rest, 8), some)
    theirs = pl.ds(pl.multiple_of((1 - here.c) * rest, 8), some)
    col_swap = to_sibling(here, col_all.at[theirs], col_sib, sib_send, sib_recv, 2)
    col_swap.start()
    col_swap.wait_recv()
    total = merged([col_all[mine, :], col_sib[...]])
    piece = some // 2
    totals_of[:] = [total[0:piece], total[piece:]]

    def col_start(stage):
        for p, order in enumerate(("zy", "yz")):
            number = 2 * stage + p
            col_sums[number, getattr(here, order[stage])] = totals_of[p]
            sums.append(Exchange(here, col_sums.at[number], small_send, small_recv, 7 + number, order[stage]))
            sums[-1].start()

    def col_wait(stage):
        for p in range(2):
            number = 2 * stage + p
            sums[7 + number].wait()
            totals_of[p] = merged([col_sums[number, k] for k in range(SIDE)])

    col_start(0)
    col_wait(0)
    col_start(1)
    right.finish()
    left.finish()
    col_wait(1)
    col_out[mine, :] = log_tgt[mine, :] - LN2 * jnp.concatenate(totals_of, axis=0)
    sent = pl.ds(pl.multiple_of(here.c * some, 8), rest)
    taken = pl.ds(pl.multiple_of((1 - here.c) * some, 8), rest)
    col_share = to_sibling(here, col_out.at[sent], col_out.at[sent], sib_send, sib_recv, 3)
    col_share.start()
    to_sibling(here, col_out.at[taken], col_out.at[taken], sib_send, sib_recv, 3).wait_recv()

    for exchange in sums:
        exchange.finish()
    for copy in (core_swap, half_swap, col_swap, col_share):
        copy.wait_send()


def plan_kernel(source_count, score, row_shift, row_in, col_in, plan, row_out, col_out, buffer, done):
    pieces = done.shape[0] - 2
    width = buffer.shape[1] // pieces
    copies = [
        pltpu.make_async_copy(row_in, row_out, done.at[pieces]),
        pltpu.make_async_copy(col_in, col_out, done.at[pieces + 1]),
    ]
    for copy in copies:
        copy.start()
    for i in range(pieces):
        for q in range(i * width // LANES, (i + 1) * width // LANES):
            at = pl.ds(q * LANES, LANES)
            shift = col_in[pl.ds(q, 1), :] * LOG2E + math.log2(source_count)
            buffer[:, at] = jnp.exp2(score[:, at] + row_shift[...] + shift)
        at = pl.ds(i * width, width)
        copies.append(pltpu.make_async_copy(buffer.at[:, at], plan.at[:, at], done.at[i]))
        copies[-1].start()
    for copy in copies:
        copy.wait()


def per_device(
    coupling,
    src_left,
    emitter_distance_rightside,
    destination_distance_leftside,
    tgt_right,
    log_src,
    logarithm_destination_masses,
    tgt_potential,
):
    rows, columns = coupling.shape
    rank = src_left.shape[1]
    col_rows = columns // LANES
    some = -(-col_rows // 32) * 16
    source_count = rows * lax.axis_size("row")
    blocks = (SIDE, SIDE, 2, SHARE, columns)
    vmem = pl.BlockSpec(memory_space=pltpu.VMEM)
    anywhere = pl.BlockSpec(memory_space=pl.ANY)
    inputs = [
        coupling,
        tgt_right,
        destination_distance_leftside,
        src_left,
        emitter_distance_rightside,
        log_src.reshape(1, rows),
        logarithm_destination_masses.reshape(col_rows, LANES),
        tgt_potential.reshape(col_rows, LANES),
    ]
    outputs = pl.pallas_call(
        main_kernel,
        name="main",
        out_shape=[
            pltpu.VMEM((rows, columns), F32),
            pltpu.VMEM((rows, LANES), F32),
            pltpu.VMEM((1, rows), F32),
            pltpu.VMEM((col_rows, LANES), F32),
        ],
        in_specs=[anywhere] * len(inputs),
        out_specs=[vmem] * 4,
        scratch_shapes=[
            pltpu.VMEM(blocks, BF16),
            pltpu.VMEM(blocks, BF16),
            pltpu.VMEM((columns, 2 * rank), BF16),
            pltpu.VMEM((rank, rank), F32),
            pltpu.VMEM((rank // 2, rank), F32),
            pltpu.VMEM((6, SIDE, rank // 4, rank), F32),
            pltpu.VMEM((2, rank // 2, rank), BF16),
            pltpu.VMEM((rows, LANES), F32),
            pltpu.VMEM((rows, LANES), F32),
            pltpu.VMEM((SIDE, 8, LANES), F32),
            pltpu.VMEM((col_rows, LANES), F32),
            pltpu.VMEM((some, LANES), F32),
            pltpu.VMEM((4, SIDE, some // 2, LANES), F32),
            pltpu.VMEM((rows, rank), BF16),
            pltpu.VMEM((rows, rank), BF16),
            pltpu.VMEM((1, rows), F32),
            pltpu.VMEM((col_rows, LANES), F32),
            pltpu.VMEM((col_rows, LANES), F32),
            pltpu.SemaphoreType.DMA((len(inputs),)),
            pltpu.SemaphoreType.DMA((Gather.SENDS,)),
            pltpu.SemaphoreType.DMA((Gather.RECEIVES,)),
            pltpu.SemaphoreType.DMA((Gather.SENDS,)),
            pltpu.SemaphoreType.DMA((Gather.RECEIVES,)),
            pltpu.SemaphoreType.DMA((11,)),
            pltpu.SemaphoreType.DMA((11,)),
            pltpu.SemaphoreType.DMA((4,)),
            pltpu.SemaphoreType.DMA((4,)),
        ],
        compiler_params=pltpu.CompilerParams(
            collective_id=0, has_side_effects=True, vmem_limit_bytes=44 * 1024 * 1024
        ),
    )(*[pltpu.with_memory_space_constraint(array, pltpu.HBM) for array in inputs])
    outputs = [pltpu.with_memory_space_constraint(array, pltpu.VMEM) for array in outputs]
    pieces = columns // step_of(columns, 768)
    plan, row_potential, col_potential = pl.pallas_call(
        functools.partial(plan_kernel, source_count),
        name="plan",
        out_shape=[
            jax.ShapeDtypeStruct((rows, columns), F32),
            jax.ShapeDtypeStruct((1, rows), F32),
            jax.ShapeDtypeStruct((col_rows, LANES), F32),
        ],
        in_specs=[vmem] * 4,
        out_specs=[anywhere] * 3,
        scratch_shapes=[pltpu.VMEM((rows, columns), F32), pltpu.SemaphoreType.DMA((pieces + 2,))],
        compiler_params=pltpu.CompilerParams(vmem_limit_bytes=32 * 1024 * 1024),
    )(*outputs)
    return plan, row_potential.reshape(rows), col_potential.reshape(columns)


def solution(mesh):
    return jax.shard_map(
        per_device,
        mesh=mesh,
        in_specs=(
            P("row", "col"),
            P("row", None),
            P("row", None),
            P("row", "col"),
            P("row", "col"),
            P("row"),
            P("col"),
            P("col"),
        ),
        out_specs=(P("row", "col"), P("row"), P("col")),
        check_vma=False,
    )
```

```python
import functools
import math

import jax
import jax.numpy as jnp
from jax import lax
from jax.experimental import pallas as pl
from jax.experimental.pallas import tpu as pltpu
from jax.sharding import PartitionSpec as P

MESH = pl.DeviceIdType.MESH
BF16 = jnp.bfloat16
F32 = jnp.float32
SIDE = 4
SHARE = 4
LANES = 128
REGULARIZATION = 4.0
LOG2E = math.log2(math.e)
LN2 = math.log(2.0)
SCORE = 2.0 / REGULARIZATION * LOG2E


def wrap(v):
    return lax.rem(v + 2 * SIDE, SIDE)


class Place:
    def __init__(self):
        row = lax.axis_index("row")
        self.x = lax.axis_index("col")
        self.y = lax.div(row, 2 * SIDE)
        self.z = lax.rem(lax.div(row, 2), SIDE)
        self.c = lax.rem(row, 2)
        self.near = {axis: {step: wrap(getattr(self, axis) + step) for step in (-1, 0, 1, 2)} for axis in "xyz"}
        self.ids = {}

    def other(self, dx=0, dy=0, dz=0, dc=0):
        key = (dx, dy, dz, dc)
        if key not in self.ids:
            core = 1 - self.c if dc else self.c
            row = (self.near["y"][dy] * SIDE + self.near["z"][dz]) * 2 + core
            self.ids[key] = {"row": row, "col": self.near["x"][dx]}
        return self.ids[key]


class Gather:
    KINDS = ("A", "B")
    RECEIVES = 41
    SENDS = 3

    def __init__(self, here, raw, send, recv):
        self.here, self.raw, self.send, self.recv = here, raw, send, recv
        columns = raw.shape[-1]
        self.half, self.quarter = columns // 2, columns // 4

    def ref(self, kind, a, b, part, core=None):
        h = self.here
        core = h.c if core is None else core
        start = 0 if kind == "A" else self.half
        if part is None:
            columns = pl.ds(start, self.half)
        else:
            columns = pl.ds(start + part * self.quarter, self.quarter)
        dy, dz = (a, b) if kind == "A" else (b, a)
        y = slice(None) if dy is None else h.near["y"][dy]
        z = slice(None) if dz is None else h.near["z"][dz]
        return self.raw.at[y, z, core, :, columns]


    def copy(self, send, receive, ref, device):
        return pltpu.make_async_remote_copy(
            src_ref=ref,
            dst_ref=ref,
            send_sem=self.send.at[send],
            recv_sem=self.recv.at[receive],
            device_id=device,
            device_id_type=MESH,
        )

    def start(self, send, receive, ref, device):
        self.copy(send, receive, ref, device).start()

    def wait(self, receive, ref):
        self.copy(0, receive, ref, self.here.other(dc=1)).wait_recv()

    def along(self, kind, first, step):
        if first == (kind == "A"):
            return self.here.other(dz=step)
        return self.here.other(dy=step)


    @staticmethod
    def side(step):
        return 0 if step == 1 else 1

    def number(self, kind, number):
        return number + (0 if kind == "A" else 20)

    def first_number(self, kind, part, step):
        return self.number(kind, part * 2 + self.side(step))

    def last_number(self, kind, b, part, step):
        ends = part != self.side(step)
        return self.number(kind, 14 + self.side(step) if ends else 8 + 2 * b + part)

    def first(self, kind, part, step):
        number = self.first_number(kind, part, step)
        self.start(0, number, self.ref(kind, 0, 0, part), self.along(kind, True, step))

    def wait_first(self, kind, part, step):
        self.wait(self.first_number(kind, part, step), self.ref(kind, 0, -step, part))

    def first_on(self, kind, step):
        part = self.side(step)
        self.start(0, self.number(kind, 4 + part), self.ref(kind, 0, -step, part), self.along(kind, True, step))

    def wait_first_on(self, kind, step):
        part = self.side(step)
        self.wait(self.number(kind, 4 + part), self.ref(kind, 0, 2, part))

    def last(self, kind, b, part, step):
        number = self.last_number(kind, b, part, step)
        self.start(1, number, self.ref(kind, 0, b, part), self.along(kind, False, step))

    def wait_last(self, kind, b, step):
        part = self.side(step)
        self.wait(self.last_number(kind, b, part, step), self.ref(kind, -step, b, part))

    def wait_ending(self, kind, step):
        part = 1 - self.side(step)
        self.wait(self.last_number(kind, 0, part, step), self.ref(kind, -step, None, part))

    def last_on(self, kind, b, step):
        part = self.side(step)
        self.start(1, self.number(kind, 17 + b), self.ref(kind, -step, b, part), self.along(kind, False, step))

    def wait_last_on(self, kind, b):
        self.wait(self.number(kind, 17 + b), self.ref(kind, 2, b, None))

    def to_sibling(self, kind, a, b, part=None):
        self.start(2, 40, self.ref(kind, a, b, part), self.here.other(dc=1))

    STEPS = ((1, 0), (-1, 1))

    def step(self, number):
        getattr(self, "step_%d" % number)()

    def step_0(self):
        for kind in self.KINDS:
            for step, part in self.STEPS:
                self.first(kind, part, step)
        for kind in self.KINDS:
            for step, part in self.STEPS:
                self.first(kind, 1 - part, step)
        for kind in self.KINDS:
            for step, part in self.STEPS:
                self.last(kind, 0, part, step)
        for kind in self.KINDS:
            for step, part in self.STEPS:
                self.last(kind, 0, 1 - part, step)

    def step_1(self):
        for kind in self.KINDS:
            for step, part in self.STEPS:
                self.wait_first(kind, part, step)
                self.first_on(kind, step)
                self.last(kind, -step, part, step)

    def step_2(self):
        for kind in self.KINDS:
            for step, part in self.STEPS:
                self.wait_first(kind, 1 - part, step)
                self.last(kind, -step, 1 - part, -step)

    def step_3(self):
        for kind in self.KINDS:
            for step, part in self.STEPS:
                self.wait_last(kind, 0, step)
                self.last_on(kind, 0, step)
        for kind in self.KINDS:
            for b in (-1, 1):
                for step, part in self.STEPS:
                    self.last(kind, b, 1 - part, step)

    def step_4(self):
        for kind in self.KINDS:
            for step, part in self.STEPS:
                self.wait_first_on(kind, step)
                self.last(kind, 2, part, step)
        for kind in self.KINDS:
            self.to_sibling(kind, 0, None)

    def step_5(self):
        for kind in self.KINDS:
            for b in (-1, 1):
                for step, part in self.STEPS:
                    self.wait_last(kind, b, step)
                    self.last_on(kind, b, step)
        for kind in self.KINDS:
            for step, part in self.STEPS:
                self.last(kind, 2, 1 - part, step)

    def step_6(self):
        for kind in self.KINDS:
            for step, part in self.STEPS:
                self.wait_last(kind, 2, step)
                self.last_on(kind, 2, step)
        for kind in self.KINDS:
            for step, part in self.STEPS:
                self.to_sibling(kind, -step, None, part)

    def step_7(self):
        for kind in self.KINDS:
            for step, part in self.STEPS:
                self.wait_ending(kind, step)
                self.to_sibling(kind, -step, None, 1 - part)

    def step_8(self):
        for b in (0, -1, 1, 2):
            for kind in self.KINDS:
                self.wait_last_on(kind, b)
                self.to_sibling(kind, 2, b)

    def step_9(self):
        self.wait(40, self.raw.at[:, :, 1 - self.here.c])

    def finish(self):
        for send, ref in enumerate((self.raw.at[0, 0:3, 0], self.raw.at[0:3, :, 0], self.raw.at[:, :, 0])):
            self.copy(send, 0, ref, self.here.other(dc=1)).wait_send()


class Exchange:
    def __init__(self, here, buffer, send, recv, axis):
        self.here, self.buffer, self.axis = here, buffer, axis
        self.send, self.recv = send, recv

    def copy(self, ref, device):
        return pltpu.make_async_remote_copy(
            src_ref=ref,
            dst_ref=ref,
            send_sem=self.send,
            recv_sem=self.recv,
            device_id=device,
            device_id_type=MESH,
        )

    def start(self):
        for step in (2, 1, -1):
            own = self.buffer.at[getattr(self.here, self.axis)]
            self.copy(own, self.here.other(**{"d" + self.axis: step})).start()

    def wait(self, three_parts=None):
        three_parts = self.buffer.at[0:3] if three_parts is None else three_parts
        self.copy(three_parts, self.here.other(dc=1)).wait_recv()

    def finish(self, three_parts):
        self.copy(three_parts, self.here.other(dc=1)).wait_send()


def to_sibling(here, src, dst, send, recv, index):
    return pltpu.make_async_remote_copy(
        src_ref=src,
        dst_ref=dst,
        send_sem=send.at[index],
        recv_sem=recv.at[index],
        device_id=here.other(dc=1),
        device_id_type=MESH,
    )


def added(parts):
    return (parts[0] + parts[1]) + (parts[2] + parts[3])


def merged(parts):
    peak = functools.reduce(jnp.maximum, parts)
    total = functools.reduce(jnp.add, [jnp.exp2(part - peak) for part in parts])
    return peak + jnp.log2(total)


def step_of(columns, most):
    return max(s for s in range(LANES, most + 1, LANES) if columns % s == 0)


def main_kernel(
    coupling_hbm, tgt_right_hbm, tgt_left_hbm,
    src_left_hbm, src_right_hbm, log_src_hbm, log_tgt_hbm, tgt_potential_hbm,
    wide, row_shift_out, row_out, col_out,
    raw_right, raw_left, image, core_part, core_sib, core_sums, core_half,
    peaks, totals, row_parts, col_all, col_sib, col_sums,
    src_left, src_right, log_src, log_tgt, tgt_potential,
    local, right_send, right_recv, left_send, left_recv,
    small_send, small_recv, sib_send, sib_recv,
):
    here = Place()
    columns = wide.shape[1]
    rows = wide.shape[0]

    barrier = pltpu.get_barrier_semaphore()
    partners = [here.other(dc=1)]
    for axis in "xyz":
        partners += [here.other(**{"d" + axis: step}) for step in (1, -1, 2)]
    for partner in partners:
        pl.semaphore_signal(barrier, inc=1, device_id=partner, device_id_type=MESH)
    loads = []
    for k, (source, target) in enumerate((
        (tgt_right_hbm, raw_right.at[here.y, here.z, here.c]),
        (src_right_hbm, src_right),
        (tgt_left_hbm, raw_left.at[here.y, here.z, here.c]),
        (coupling_hbm, wide),
        (src_left_hbm, src_left),
        (log_src_hbm, log_src),
        (log_tgt_hbm, log_tgt),
        (tgt_potential_hbm, tgt_potential),
    )):
        loads.append(pltpu.make_async_copy(source, target, local.at[k]))
        loads[-1].start()

    loads[0].wait()
    pl.semaphore_wait(barrier, len(partners))

    right = Gather(here, raw_right, right_send, right_recv)
    left = Gather(here, raw_left, left_send, left_recv)
    right.step(0)

    for k in (1, 2, 3):
        loads[k].wait()
    side = jnp.concatenate([src_right[...], src_right[...]], axis=0)
    width = step_of(columns, 3072)

    def image_step(i, _):
        at = pl.ds(pl.multiple_of(i * width, width), width)
        entries = wide[:, at]
        high = entries.astype(BF16)
        low = (entries - high.astype(F32)).astype(BF16)
        value = lax.dot_general(
            jnp.concatenate([high, low], axis=0), side, (((0,), (0,)), ((), ())), preferred_element_type=F32
        )
        value_high = value.astype(BF16)
        image[at, 0:LANES] = value_high
        image[at, LANES : 2 * LANES] = (value - value_high.astype(F32)).astype(BF16)
        return 0

    steps = columns // width
    cuts = [0, 0, (steps * 2) // 5, (steps * 3) // 5, steps]
    for k in range(4):
        lax.fori_loop(cuts[k], cuts[k + 1], image_step, 0)
        right.step(k + 1)
    right.step(5)
    left.step(0)
    right.step(6)
    right.step(7)
    right.step(8)
    left.step(1)
    left.step(2)
    right.step(9)

    factor = raw_right[...].reshape(LANES, columns)
    parts = jnp.dot(factor, image[...], preferred_element_type=F32)
    core_part[...] = parts[:, 0:LANES] + parts[:, LANES : 2 * LANES]

    part_rows = LANES // 2
    mine = pl.ds(pl.multiple_of(here.c * part_rows, part_rows), part_rows)
    theirs = pl.ds(pl.multiple_of((1 - here.c) * part_rows, part_rows), part_rows)
    core_swap = to_sibling(here, core_part.at[theirs], core_sib, sib_send, sib_recv, 0)
    core_swap.start()
    left.step(3)
    core_swap.wait_recv()
    total = core_part[mine] + core_sib[...]
    piece = part_rows // 2
    totals_of = [total[0:piece], total[piece:]]
    sums = []

    def sum_start(stage):
        for p, order in enumerate(("xyz", "yzx")):
            number = 2 * stage + p
            core_sums[number, getattr(here, order[stage])] = totals_of[p]
            sums.append(Exchange(here, core_sums.at[number], small_send.at[0], small_recv.at[stage], order[stage]))
            sums[-1].start()

    def sum_wait(stage):
        sums[2 * stage].wait(core_sums.at[2 * stage : 2 * stage + 2, 0:3])
        for p in range(2):
            number = 2 * stage + p
            totals_of[p] = added([core_sums[number, k] for k in range(SIDE)])

    sum_start(0)
    left.step(4)
    left.step(5)
    sum_wait(0)
    sum_start(1)
    left.step(6)
    left.step(7)
    sum_wait(1)
    sum_start(2)
    left.step(8)
    sum_wait(2)
    core_half[here.c] = jnp.concatenate(totals_of, axis=0).astype(BF16)
    half_swap = to_sibling(here, core_half.at[here.c], core_half.at[here.c], sib_send, sib_recv, 1)
    half_swap.start()
    for k in range(4, 8):
        loads[k].wait()
    left.step(9)
    to_sibling(here, core_half.at[1 - here.c], core_half.at[1 - here.c], sib_send, sib_recv, 1).wait_recv()
    core = core_half[...].reshape(LANES, LANES)
    rows_cost = lax.dot_general(
        src_left[...], core, (((1,), (1,)), ((), ())), preferred_element_type=F32
    ).astype(BF16)

    span = step_of(columns, 7680)

    peaks[...] = jnp.full_like(peaks, -jnp.inf)
    tiles = span // LANES

    def score_step(i, _):
        at = pl.ds(pl.multiple_of(i * span, span), span)
        factor = raw_left[:, :, :, :, at].reshape(LANES, span)
        score = jnp.dot(rows_cost, factor, preferred_element_type=F32) * SCORE
        wide[:, at] = score
        peak = peaks[...]
        for q in range(tiles):
            shift = tgt_potential[pl.ds(i * tiles + q, 1), :] * LOG2E
            peak = jnp.maximum(peak, score[:, q * LANES : (q + 1) * LANES] + shift)
        peaks[...] = peak
        return 0

    lax.fori_loop(0, columns // span, score_step, 0)

    totals[...] = jnp.zeros_like(totals)
    reach = step_of(columns, 3072)
    pieces = reach // LANES

    def total_step(i, _):
        peak = peaks[...]
        total = totals[...]
        for q in range(pieces):
            at = pl.ds(pl.multiple_of(i * reach + q * LANES, LANES), LANES)
            shift = tgt_potential[pl.ds(i * pieces + q, 1), :] * LOG2E
            total = total + jnp.exp2(wide[:, at] + shift - peak)
        totals[...] = total
        return 0

    lax.fori_loop(0, columns // reach, total_step, 0)
    lane_peak = peaks[...].T
    row_peak = jnp.max(lane_peak, axis=0, keepdims=True)
    row_total = jnp.sum(totals[...].T * jnp.exp2(lane_peak - row_peak), axis=0, keepdims=True)
    row_parts[here.x] = jnp.broadcast_to(row_peak + jnp.log2(row_total), row_parts.shape[1:])
    rows_x = Exchange(here, row_parts, small_send.at[1], small_recv.at[3], "x")
    sums.append(rows_x)
    rows_x.start()
    rows_x.wait()
    row_sum = merged([row_parts[k] for k in range(SIDE)])[0:1]
    row_potential = log_src[...] - LN2 * row_sum
    row_out[...] = row_potential
    row_shift_out[...] = jnp.broadcast_to(row_potential * LOG2E, (LANES, LANES)).T

    def col_step(i, _):
        for q in range(pieces):
            at = pl.ds(pl.multiple_of(i * reach + q * LANES, LANES), LANES)
            score = (wide[:, at] + row_shift_out[...]).reshape(rows // 8, 8, LANES)
            peak = jnp.max(score, axis=0)
            total = jnp.sum(jnp.exp2(score - peak[None]), axis=0)
            top = jnp.max(peak, axis=0, keepdims=True)
            total = jnp.sum(total * jnp.exp2(peak - top), axis=0, keepdims=True)
            col_all[pl.ds(i * pieces + q, 1), :] = top + jnp.log2(total)
        return 0

    lax.fori_loop(0, columns // reach, col_step, 0)

    col_rows = col_all.shape[0]
    some = col_sib.shape[0]
    rest = col_rows - some
    mine = pl.ds(pl.multiple_of(here.c * rest, 8), some)
    theirs = pl.ds(pl.multiple_of((1 - here.c) * rest, 8), some)
    col_swap = to_sibling(here, col_all.at[theirs], col_sib, sib_send, sib_recv, 2)
    col_swap.start()
    col_swap.wait_recv()
    total = merged([col_all[mine, :], col_sib[...]])
    piece = some // 2
    totals_of[:] = [total[0:piece], total[piece:]]

    def col_start(stage):
        for p, order in enumerate(("zy", "yz")):
            number = 2 * stage + p
            col_sums[number, getattr(here, order[stage])] = totals_of[p]
            sums.append(Exchange(here, col_sums.at[number], small_send.at[2], small_recv.at[4 + stage], order[stage]))
            sums[-1].start()

    def col_wait(stage):
        sums[7 + 2 * stage].wait(col_sums.at[2 * stage : 2 * stage + 2, 0:3])
        for p in range(2):
            number = 2 * stage + p
            totals_of[p] = merged([col_sums[number, k] for k in range(SIDE)])

    col_start(0)
    col_wait(0)
    col_start(1)
    right.finish()
    left.finish()
    col_wait(1)
    col_out[mine, :] = log_tgt[mine, :] - LN2 * jnp.concatenate(totals_of, axis=0)
    sent = pl.ds(pl.multiple_of(here.c * some, 8), rest)
    taken = pl.ds(pl.multiple_of((1 - here.c) * some, 8), rest)
    col_share = to_sibling(here, col_out.at[sent], col_out.at[sent], sib_send, sib_recv, 3)
    col_share.start()
    to_sibling(here, col_out.at[taken], col_out.at[taken], sib_send, sib_recv, 3).wait_recv()

    sums[0].finish(core_sums.at[:, 0:3])
    rows_x.finish(row_parts.at[0:3])
    sums[7].finish(col_sums.at[:, 0:3])
    for copy in (core_swap, half_swap, col_swap, col_share):
        copy.wait_send()


def plan_kernel(source_count, score, row_shift, row_in, col_in, plan, row_out, col_out, buffer, done):
    pieces = done.shape[0] - 2
    width = buffer.shape[1] // pieces
    copies = [
        pltpu.make_async_copy(row_in, row_out, done.at[pieces]),
        pltpu.make_async_copy(col_in, col_out, done.at[pieces + 1]),
    ]
    for copy in copies:
        copy.start()
    for i in range(pieces):
        for q in range(i * width // LANES, (i + 1) * width // LANES):
            at = pl.ds(q * LANES, LANES)
            shift = col_in[pl.ds(q, 1), :] * LOG2E + math.log2(source_count)
            buffer[:, at] = jnp.exp2(score[:, at] + row_shift[...] + shift)
        at = pl.ds(i * width, width)
        copies.append(pltpu.make_async_copy(buffer.at[:, at], plan.at[:, at], done.at[i]))
        copies[-1].start()
    for copy in copies:
        copy.wait()


def per_device(
    coupling,
    src_left,
    emitter_distance_rightside,
    destination_distance_leftside,
    tgt_right,
    log_src,
    logarithm_destination_masses,
    tgt_potential,
):
    rows, columns = coupling.shape
    rank = src_left.shape[1]
    col_rows = columns // LANES
    some = -(-col_rows // 32) * 16
    source_count = rows * lax.axis_size("row")
    blocks = (SIDE, SIDE, 2, SHARE, columns)
    vmem = pl.BlockSpec(memory_space=pltpu.VMEM)
    anywhere = pl.BlockSpec(memory_space=pl.ANY)
    inputs = [
        coupling,
        tgt_right,
        destination_distance_leftside,
        src_left,
        emitter_distance_rightside,
        log_src.reshape(1, rows),
        logarithm_destination_masses.reshape(col_rows, LANES),
        tgt_potential.reshape(col_rows, LANES),
    ]
    outputs = pl.pallas_call(
        main_kernel,
        name="main",
        out_shape=[
            pltpu.VMEM((rows, columns), F32),
            pltpu.VMEM((rows, LANES), F32),
            pltpu.VMEM((1, rows), F32),
            pltpu.VMEM((col_rows, LANES), F32),
        ],
        in_specs=[anywhere] * len(inputs),
        out_specs=[vmem] * 4,
        scratch_shapes=[
            pltpu.VMEM(blocks, BF16),
            pltpu.VMEM(blocks, BF16),
            pltpu.VMEM((columns, 2 * rank), BF16),
            pltpu.VMEM((rank, rank), F32),
            pltpu.VMEM((rank // 2, rank), F32),
            pltpu.VMEM((6, SIDE, rank // 4, rank), F32),
            pltpu.VMEM((2, rank // 2, rank), BF16),
            pltpu.VMEM((rows, LANES), F32),
            pltpu.VMEM((rows, LANES), F32),
            pltpu.VMEM((SIDE, 8, LANES), F32),
            pltpu.VMEM((col_rows, LANES), F32),
            pltpu.VMEM((some, LANES), F32),
            pltpu.VMEM((4, SIDE, some // 2, LANES), F32),
            pltpu.VMEM((rows, rank), BF16),
            pltpu.VMEM((rows, rank), BF16),
            pltpu.VMEM((1, rows), F32),
            pltpu.VMEM((col_rows, LANES), F32),
            pltpu.VMEM((col_rows, LANES), F32),
            pltpu.SemaphoreType.DMA((len(inputs),)),
            pltpu.SemaphoreType.DMA((Gather.SENDS,)),
            pltpu.SemaphoreType.DMA((Gather.RECEIVES,)),
            pltpu.SemaphoreType.DMA((Gather.SENDS,)),
            pltpu.SemaphoreType.DMA((Gather.RECEIVES,)),
            pltpu.SemaphoreType.DMA((3,)),
            pltpu.SemaphoreType.DMA((6,)),
            pltpu.SemaphoreType.DMA((4,)),
            pltpu.SemaphoreType.DMA((4,)),
        ],
        compiler_params=pltpu.CompilerParams(
            collective_id=0, has_side_effects=True, vmem_limit_bytes=44 * 1024 * 1024
        ),
    )(*[pltpu.with_memory_space_constraint(array, pltpu.HBM) for array in inputs])
    outputs = [pltpu.with_memory_space_constraint(array, pltpu.VMEM) for array in outputs]
    pieces = columns // step_of(columns, 768)
    plan, row_potential, col_potential = pl.pallas_call(
        functools.partial(plan_kernel, source_count),
        name="plan",
        out_shape=[
            jax.ShapeDtypeStruct((rows, columns), F32),
            jax.ShapeDtypeStruct((1, rows), F32),
            jax.ShapeDtypeStruct((col_rows, LANES), F32),
        ],
        in_specs=[vmem] * 4,
        out_specs=[anywhere] * 3,
        scratch_shapes=[pltpu.VMEM((rows, columns), F32), pltpu.SemaphoreType.DMA((pieces + 2,))],
        compiler_params=pltpu.CompilerParams(vmem_limit_bytes=32 * 1024 * 1024),
    )(*outputs)
    return plan, row_potential.reshape(rows), col_potential.reshape(columns)


def solution(mesh):
    return jax.shard_map(
        per_device,
        mesh=mesh,
        in_specs=(
            P("row", "col"),
            P("row", None),
            P("row", None),
            P("row", "col"),
            P("row", "col"),
            P("row"),
            P("col"),
            P("col"),
        ),
        out_specs=(P("row", "col"), P("row"), P("col")),
        check_vma=False,
    )
```

```python
import functools
import math

import jax
import jax.numpy as jnp
from jax import lax
from jax.experimental import pallas as pl
from jax.experimental.pallas import tpu as pltpu
from jax.sharding import PartitionSpec as P

MESH = pl.DeviceIdType.MESH
BF16 = jnp.bfloat16
F32 = jnp.float32
SIDE = 4
SHARE = 4
LANES = 128
REGULARIZATION = 4.0
LOG2E = math.log2(math.e)
LN2 = math.log(2.0)
SCORE = 2.0 / REGULARIZATION * LOG2E


def wrap(v):
    return lax.rem(v + 2 * SIDE, SIDE)


class Place:
    def __init__(self):
        row = lax.axis_index("row")
        self.x = lax.axis_index("col")
        self.y = lax.div(row, 2 * SIDE)
        self.z = lax.rem(lax.div(row, 2), SIDE)
        self.c = lax.rem(row, 2)
        self.near = {axis: {step: wrap(getattr(self, axis) + step) for step in (-1, 0, 1, 2)} for axis in "xyz"}
        self.ids = {}

    def other(self, dx=0, dy=0, dz=0, dc=0):
        key = (dx, dy, dz, dc)
        if key not in self.ids:
            core = 1 - self.c if dc else self.c
            row = (self.near["y"][dy] * SIDE + self.near["z"][dz]) * 2 + core
            self.ids[key] = {"row": row, "col": self.near["x"][dx]}
        return self.ids[key]


class Gather:
    KINDS = ("A", "B")
    RECEIVES = 41
    SENDS = 3

    def __init__(self, here, raw, send, recv):
        self.here, self.raw, self.send, self.recv = here, raw, send, recv
        columns = raw.shape[-1]
        self.half, self.quarter = columns // 2, columns // 4

    def ref(self, kind, a, b, part, core=None):
        h = self.here
        core = h.c if core is None else core
        start = 0 if kind == "A" else self.half
        if part is None:
            columns = pl.ds(start, self.half)
        else:
            columns = pl.ds(start + part * self.quarter, self.quarter)
        dy, dz = (a, b) if kind == "A" else (b, a)
        y = slice(None) if dy is None else h.near["y"][dy]
        z = slice(None) if dz is None else h.near["z"][dz]
        return self.raw.at[y, z, core, :, columns]


    def copy(self, send, receive, ref, device):
        return pltpu.make_async_remote_copy(
            src_ref=ref,
            dst_ref=ref,
            send_sem=self.send.at[send],
            recv_sem=self.recv.at[receive],
            device_id=device,
            device_id_type=MESH,
        )

    def start(self, send, receive, ref, device):
        self.copy(send, receive, ref, device).start()

    def wait(self, receive, ref):
        self.copy(0, receive, ref, self.here.other(dc=1)).wait_recv()

    def along(self, kind, first, step):
        if first == (kind == "A"):
            return self.here.other(dz=step)
        return self.here.other(dy=step)


    @staticmethod
    def side(step):
        return 0 if step == 1 else 1

    def number(self, kind, number):
        return number + (0 if kind == "A" else 20)

    def first_number(self, kind, part, step):
        return self.number(kind, part * 2 + self.side(step))

    def last_number(self, kind, b, part, step):
        ends = part != self.side(step)
        return self.number(kind, 14 + self.side(step) if ends else 8 + 2 * b + part)

    def first(self, kind, part, step):
        number = self.first_number(kind, part, step)
        self.start(0, number, self.ref(kind, 0, 0, part), self.along(kind, True, step))

    def wait_first(self, kind, part, step):
        self.wait(self.first_number(kind, part, step), self.ref(kind, 0, -step, part))

    def first_on(self, kind, step):
        part = self.side(step)
        self.start(0, self.number(kind, 4 + part), self.ref(kind, 0, -step, part), self.along(kind, True, step))

    def wait_first_on(self, kind, step):
        part = self.side(step)
        self.wait(self.number(kind, 4 + part), self.ref(kind, 0, 2, part))

    def last(self, kind, b, part, step):
        number = self.last_number(kind, b, part, step)
        self.start(1, number, self.ref(kind, 0, b, part), self.along(kind, False, step))

    def wait_last(self, kind, b, step):
        part = self.side(step)
        self.wait(self.last_number(kind, b, part, step), self.ref(kind, -step, b, part))

    def wait_ending(self, kind, step):
        part = 1 - self.side(step)
        self.wait(self.last_number(kind, 0, part, step), self.ref(kind, -step, None, part))

    def last_on(self, kind, b, step):
        part = self.side(step)
        self.start(1, self.number(kind, 17 + b), self.ref(kind, -step, b, part), self.along(kind, False, step))

    def wait_last_on(self, kind, b):
        self.wait(self.number(kind, 17 + b), self.ref(kind, 2, b, None))

    def to_sibling(self, kind, a, b, part=None):
        self.start(2, 40, self.ref(kind, a, b, part), self.here.other(dc=1))

    STEPS = ((1, 0), (-1, 1))

    def step(self, number):
        getattr(self, "step_%d" % number)()

    def step_0(self):
        for kind in self.KINDS:
            for step, part in self.STEPS:
                self.first(kind, part, step)
        for kind in self.KINDS:
            for step, part in self.STEPS:
                self.first(kind, 1 - part, step)
        for kind in self.KINDS:
            for step, part in self.STEPS:
                self.last(kind, 0, part, step)
        for kind in self.KINDS:
            for step, part in self.STEPS:
                self.last(kind, 0, 1 - part, step)

    def step_1(self):
        for kind in self.KINDS:
            for step, part in self.STEPS:
                self.wait_first(kind, part, step)
                self.first_on(kind, step)
                self.last(kind, -step, part, step)

    def step_2(self):
        for kind in self.KINDS:
            for step, part in self.STEPS:
                self.wait_first(kind, 1 - part, step)
                self.last(kind, -step, 1 - part, -step)

    def step_3(self):
        for kind in self.KINDS:
            for step, part in self.STEPS:
                self.wait_last(kind, 0, step)
                self.last_on(kind, 0, step)
        for kind in self.KINDS:
            for b in (-1, 1):
                for step, part in self.STEPS:
                    self.last(kind, b, 1 - part, step)

    def step_4(self):
        for kind in self.KINDS:
            for step, part in self.STEPS:
                self.wait_first_on(kind, step)
                self.last(kind, 2, part, step)
        for kind in self.KINDS:
            self.to_sibling(kind, 0, None)

    def step_5(self):
        for kind in self.KINDS:
            for b in (-1, 1):
                for step, part in self.STEPS:
                    self.wait_last(kind, b, step)
                    self.last_on(kind, b, step)
        for kind in self.KINDS:
            for step, part in self.STEPS:
                self.last(kind, 2, 1 - part, step)

    def step_6(self):
        for kind in self.KINDS:
            for step, part in self.STEPS:
                self.wait_last(kind, 2, step)
                self.last_on(kind, 2, step)
        for kind in self.KINDS:
            for step, part in self.STEPS:
                self.to_sibling(kind, -step, None, part)

    def step_7(self):
        for kind in self.KINDS:
            for step, part in self.STEPS:
                self.wait_ending(kind, step)
                self.to_sibling(kind, -step, None, 1 - part)

    def step_8(self):
        for b in (0, -1, 1, 2):
            for kind in self.KINDS:
                self.wait_last_on(kind, b)
                self.to_sibling(kind, 2, b)

    def step_9(self):
        self.wait(40, self.raw.at[:, :, 1 - self.here.c])

    def finish(self):
        for send, ref in enumerate((self.raw.at[0, 0:3, 0], self.raw.at[0:3, :, 0], self.raw.at[:, :, 0])):
            self.copy(send, 0, ref, self.here.other(dc=1)).wait_send()


class Exchange:
    def __init__(self, here, buffer, send, recv, number, axis):
        self.here, self.buffer, self.axis = here, buffer, axis
        self.send, self.recv = send.at[number], recv.at[number]

    def copy(self, ref, device):
        return pltpu.make_async_remote_copy(
            src_ref=ref,
            dst_ref=ref,
            send_sem=self.send,
            recv_sem=self.recv,
            device_id=device,
            device_id_type=MESH,
        )

    def start(self):
        for step in (2, 1, -1):
            own = self.buffer.at[getattr(self.here, self.axis)]
            self.copy(own, self.here.other(**{"d" + self.axis: step})).start()

    def wait(self):
        self.copy(self.buffer.at[0:3], self.here.other(dc=1)).wait_recv()

    def finish(self):
        self.copy(self.buffer.at[0:3], self.here.other(dc=1)).wait_send()


def to_sibling(here, src, dst, send, recv, index):
    return pltpu.make_async_remote_copy(
        src_ref=src,
        dst_ref=dst,
        send_sem=send.at[index],
        recv_sem=recv.at[index],
        device_id=here.other(dc=1),
        device_id_type=MESH,
    )


def added(parts):
    return (parts[0] + parts[1]) + (parts[2] + parts[3])


def merged(parts):
    peak = functools.reduce(jnp.maximum, parts)
    total = functools.reduce(jnp.add, [jnp.exp2(part - peak) for part in parts])
    return peak + jnp.log2(total)


def step_of(columns, most):
    return max(s for s in range(LANES, most + 1, LANES) if columns % s == 0)


def main_kernel(
    coupling_hbm, tgt_right_hbm, tgt_left_hbm,
    src_left_hbm, src_right_hbm, log_src_hbm, log_tgt_hbm, tgt_potential_hbm,
    wide, row_shift_out, row_out, col_out,
    raw_right, raw_left, image, core_part, core_sib, core_sums, core_half,
    peaks, totals, row_parts, col_all, col_sib, col_sums,
    src_left, src_right, log_src, log_tgt, tgt_potential,
    local, right_send, right_recv, left_send, left_recv,
    small_send, small_recv, sib_send, sib_recv,
):
    here = Place()
    columns = wide.shape[1]
    rows = wide.shape[0]

    barrier = pltpu.get_barrier_semaphore()
    partners = [here.other(dc=1)]
    for axis in "xyz":
        partners += [here.other(**{"d" + axis: step}) for step in (1, -1, 2)]
    for partner in partners:
        pl.semaphore_signal(barrier, inc=1, device_id=partner, device_id_type=MESH)
    loads = []
    for k, (source, target) in enumerate((
        (tgt_right_hbm, raw_right.at[here.y, here.z, here.c]),
        (src_right_hbm, src_right),
        (tgt_left_hbm, raw_left.at[here.y, here.z, here.c]),
        (coupling_hbm, wide),
        (src_left_hbm, src_left),
        (log_src_hbm, log_src),
        (log_tgt_hbm, log_tgt),
        (tgt_potential_hbm, tgt_potential),
    )):
        loads.append(pltpu.make_async_copy(source, target, local.at[k]))
        loads[-1].start()

    loads[0].wait()
    pl.semaphore_wait(barrier, len(partners))

    right = Gather(here, raw_right, right_send, right_recv)
    left = Gather(here, raw_left, left_send, left_recv)
    right.step(0)

    for k in (1, 2, 3):
        loads[k].wait()
    side = jnp.concatenate([src_right[...], src_right[...]], axis=0)
    width = step_of(columns, 3072)

    def image_step(i, _):
        at = pl.ds(pl.multiple_of(i * width, width), width)
        entries = wide[:, at]
        high = entries.astype(BF16)
        low = (entries - high.astype(F32)).astype(BF16)
        value = lax.dot_general(
            jnp.concatenate([high, low], axis=0), side, (((0,), (0,)), ((), ())), preferred_element_type=F32
        )
        value_high = value.astype(BF16)
        image[at, 0:LANES] = value_high
        image[at, LANES : 2 * LANES] = (value - value_high.astype(F32)).astype(BF16)
        return 0

    steps = columns // width
    cuts = [0, 0, (steps * 2) // 5, (steps * 3) // 5, steps]
    for k in range(4):
        lax.fori_loop(cuts[k], cuts[k + 1], image_step, 0)
        right.step(k + 1)
    right.step(5)
    left.step(0)
    right.step(6)
    right.step(7)
    right.step(8)
    left.step(1)
    left.step(2)
    right.step(9)

    factor = raw_right[...].reshape(LANES, columns)
    parts = jnp.dot(factor, image[...], preferred_element_type=F32)
    core_part[...] = parts[:, 0:LANES] + parts[:, LANES : 2 * LANES]

    part_rows = LANES // 2
    mine = pl.ds(pl.multiple_of(here.c * part_rows, part_rows), part_rows)
    theirs = pl.ds(pl.multiple_of((1 - here.c) * part_rows, part_rows), part_rows)
    core_swap = to_sibling(here, core_part.at[theirs], core_sib, sib_send, sib_recv, 0)
    core_swap.start()
    left.step(3)
    core_swap.wait_recv()
    total = core_part[mine] + core_sib[...]
    piece = part_rows // 2
    totals_of = [total[0:piece], total[piece:]]
    sums = []

    def sum_start(stage):
        for p, order in enumerate(("xyz", "yzx")):
            number = 2 * stage + p
            core_sums[number, getattr(here, order[stage])] = totals_of[p]
            sums.append(Exchange(here, core_sums.at[number], small_send, small_recv, number, order[stage]))
            sums[-1].start()

    def sum_wait(stage):
        for p in range(2):
            number = 2 * stage + p
            sums[number].wait()
            totals_of[p] = added([core_sums[number, k] for k in range(SIDE)])

    sum_start(0)
    left.step(4)
    left.step(5)
    sum_wait(0)
    sum_start(1)
    left.step(6)
    left.step(7)
    sum_wait(1)
    sum_start(2)
    left.step(8)
    sum_wait(2)
    core_half[here.c] = jnp.concatenate(totals_of, axis=0).astype(BF16)
    half_swap = to_sibling(here, core_half.at[here.c], core_half.at[here.c], sib_send, sib_recv, 1)
    half_swap.start()
    for k in range(4, 8):
        loads[k].wait()
    left.step(9)
    to_sibling(here, core_half.at[1 - here.c], core_half.at[1 - here.c], sib_send, sib_recv, 1).wait_recv()
    core = core_half[...].reshape(LANES, LANES)
    rows_cost = lax.dot_general(
        src_left[...], core, (((1,), (1,)), ((), ())), preferred_element_type=F32
    ).astype(BF16)

    span = step_of(columns, 5120)

    peaks[...] = jnp.full_like(peaks, -jnp.inf)
    tiles = span // LANES

    def score_step(i, _):
        at = pl.ds(pl.multiple_of(i * span, span), span)
        factor = raw_left[:, :, :, :, at].reshape(LANES, span)
        score = jnp.dot(rows_cost, factor, preferred_element_type=F32) * SCORE
        wide[:, at] = score
        peak = peaks[...]
        for q in range(tiles):
            shift = tgt_potential[pl.ds(i * tiles + q, 1), :] * LOG2E
            peak = jnp.maximum(peak, score[:, q * LANES : (q + 1) * LANES] + shift)
        peaks[...] = peak
        return 0

    lax.fori_loop(0, columns // span, score_step, 0)

    totals[...] = jnp.zeros_like(totals)
    reach = step_of(columns, 3072)
    pieces = reach // LANES

    def total_step(i, _):
        peak = peaks[...]
        total = totals[...]
        for q in range(pieces):
            at = pl.ds(pl.multiple_of(i * reach + q * LANES, LANES), LANES)
            shift = tgt_potential[pl.ds(i * pieces + q, 1), :] * LOG2E
            total = total + jnp.exp2(wide[:, at] + shift - peak)
        totals[...] = total
        return 0

    lax.fori_loop(0, columns // reach, total_step, 0)
    lane_peak = peaks[...].T
    row_peak = jnp.max(lane_peak, axis=0, keepdims=True)
    row_total = jnp.sum(totals[...].T * jnp.exp2(lane_peak - row_peak), axis=0, keepdims=True)
    row_parts[here.x] = jnp.broadcast_to(row_peak + jnp.log2(row_total), row_parts.shape[1:])
    rows_x = Exchange(here, row_parts, small_send, small_recv, 6, "x")
    sums.append(rows_x)
    rows_x.start()
    rows_x.wait()
    row_sum = merged([row_parts[k] for k in range(SIDE)])[0:1]
    row_potential = log_src[...] - LN2 * row_sum
    row_out[...] = row_potential
    row_shift_out[...] = jnp.broadcast_to(row_potential * LOG2E, (LANES, LANES)).T

    def col_step(i, _):
        for q in range(pieces):
            at = pl.ds(pl.multiple_of(i * reach + q * LANES, LANES), LANES)
            score = (wide[:, at] + row_shift_out[...]).reshape(rows // 8, 8, LANES)
            peak = jnp.max(score, axis=0)
            total = jnp.sum(jnp.exp2(score - peak[None]), axis=0)
            top = jnp.max(peak, axis=0, keepdims=True)
            total = jnp.sum(total * jnp.exp2(peak - top), axis=0, keepdims=True)
            col_all[pl.ds(i * pieces + q, 1), :] = top + jnp.log2(total)
        return 0

    lax.fori_loop(0, columns // reach, col_step, 0)

    col_rows = col_all.shape[0]
    some = col_sib.shape[0]
    rest = col_rows - some
    mine = pl.ds(pl.multiple_of(here.c * rest, 8), some)
    theirs = pl.ds(pl.multiple_of((1 - here.c) * rest, 8), some)
    col_swap = to_sibling(here, col_all.at[theirs], col_sib, sib_send, sib_recv, 2)
    col_swap.start()
    col_swap.wait_recv()
    total = merged([col_all[mine, :], col_sib[...]])
    piece = some // 2
    totals_of[:] = [total[0:piece], total[piece:]]

    def col_start(stage):
        for p, order in enumerate(("zy", "yz")):
            number = 2 * stage + p
            col_sums[number, getattr(here, order[stage])] = totals_of[p]
            sums.append(Exchange(here, col_sums.at[number], small_send, small_recv, 7 + number, order[stage]))
            sums[-1].start()

    def col_wait(stage):
        for p in range(2):
            number = 2 * stage + p
            sums[7 + number].wait()
            totals_of[p] = merged([col_sums[number, k] for k in range(SIDE)])

    col_start(0)
    col_wait(0)
    col_start(1)
    right.finish()
    left.finish()
    col_wait(1)
    col_out[mine, :] = log_tgt[mine, :] - LN2 * jnp.concatenate(totals_of, axis=0)
    sent = pl.ds(pl.multiple_of(here.c * some, 8), rest)
    taken = pl.ds(pl.multiple_of((1 - here.c) * some, 8), rest)
    col_share = to_sibling(here, col_out.at[sent], col_out.at[sent], sib_send, sib_recv, 3)
    col_share.start()
    to_sibling(here, col_out.at[taken], col_out.at[taken], sib_send, sib_recv, 3).wait_recv()

    for exchange in sums:
        exchange.finish()
    for copy in (core_swap, half_swap, col_swap, col_share):
        copy.wait_send()


def plan_kernel(source_count, score, row_shift, row_in, col_in, plan, row_out, col_out, buffer, done):
    pieces = done.shape[0] - 2
    width = buffer.shape[1] // pieces
    copies = [
        pltpu.make_async_copy(row_in, row_out, done.at[pieces]),
        pltpu.make_async_copy(col_in, col_out, done.at[pieces + 1]),
    ]
    for copy in copies:
        copy.start()
    for i in range(pieces):
        for q in range(i * width // LANES, (i + 1) * width // LANES):
            at = pl.ds(q * LANES, LANES)
            shift = col_in[pl.ds(q, 1), :] * LOG2E + math.log2(source_count)
            buffer[:, at] = jnp.exp2(score[:, at] + row_shift[...] + shift)
        at = pl.ds(i * width, width)
        copies.append(pltpu.make_async_copy(buffer.at[:, at], plan.at[:, at], done.at[i]))
        copies[-1].start()
    for copy in copies:
        copy.wait()


def per_device(
    coupling,
    src_left,
    emitter_distance_rightside,
    destination_distance_leftside,
    tgt_right,
    log_src,
    logarithm_destination_masses,
    tgt_potential,
):
    rows, columns = coupling.shape
    rank = src_left.shape[1]
    col_rows = columns // LANES
    some = -(-col_rows // 32) * 16
    source_count = rows * lax.axis_size("row")
    blocks = (SIDE, SIDE, 2, SHARE, columns)
    vmem = pl.BlockSpec(memory_space=pltpu.VMEM)
    anywhere = pl.BlockSpec(memory_space=pl.ANY)
    inputs = [
        coupling,
        tgt_right,
        destination_distance_leftside,
        src_left,
        emitter_distance_rightside,
        log_src.reshape(1, rows),
        logarithm_destination_masses.reshape(col_rows, LANES),
        tgt_potential.reshape(col_rows, LANES),
    ]
    outputs = pl.pallas_call(
        main_kernel,
        name="main",
        out_shape=[
            pltpu.VMEM((rows, columns), F32),
            pltpu.VMEM((rows, LANES), F32),
            pltpu.VMEM((1, rows), F32),
            pltpu.VMEM((col_rows, LANES), F32),
        ],
        in_specs=[anywhere] * len(inputs),
        out_specs=[vmem] * 4,
        scratch_shapes=[
            pltpu.VMEM(blocks, BF16),
            pltpu.VMEM(blocks, BF16),
            pltpu.VMEM((columns, 2 * rank), BF16),
            pltpu.VMEM((rank, rank), F32),
            pltpu.VMEM((rank // 2, rank), F32),
            pltpu.VMEM((6, SIDE, rank // 4, rank), F32),
            pltpu.VMEM((2, rank // 2, rank), BF16),
            pltpu.VMEM((rows, LANES), F32),
            pltpu.VMEM((rows, LANES), F32),
            pltpu.VMEM((SIDE, 1, LANES), F32),
            pltpu.VMEM((col_rows, LANES), F32),
            pltpu.VMEM((some, LANES), F32),
            pltpu.VMEM((4, SIDE, some // 2, LANES), F32),
            pltpu.VMEM((rows, rank), BF16),
            pltpu.VMEM((rows, rank), BF16),
            pltpu.VMEM((1, rows), F32),
            pltpu.VMEM((col_rows, LANES), F32),
            pltpu.VMEM((col_rows, LANES), F32),
            pltpu.SemaphoreType.DMA((len(inputs),)),
            pltpu.SemaphoreType.DMA((Gather.SENDS,)),
            pltpu.SemaphoreType.DMA((Gather.RECEIVES,)),
            pltpu.SemaphoreType.DMA((Gather.SENDS,)),
            pltpu.SemaphoreType.DMA((Gather.RECEIVES,)),
            pltpu.SemaphoreType.DMA((11,)),
            pltpu.SemaphoreType.DMA((11,)),
            pltpu.SemaphoreType.DMA((4,)),
            pltpu.SemaphoreType.DMA((4,)),
        ],
        compiler_params=pltpu.CompilerParams(
            collective_id=0, has_side_effects=True, vmem_limit_bytes=44 * 1024 * 1024
        ),
    )(*[pltpu.with_memory_space_constraint(array, pltpu.HBM) for array in inputs])
    outputs = [pltpu.with_memory_space_constraint(array, pltpu.VMEM) for array in outputs]
    pieces = columns // step_of(columns, 768)
    plan, row_potential, col_potential = pl.pallas_call(
        functools.partial(plan_kernel, source_count),
        name="plan",
        out_shape=[
            jax.ShapeDtypeStruct((rows, columns), F32),
            jax.ShapeDtypeStruct((1, rows), F32),
            jax.ShapeDtypeStruct((col_rows, LANES), F32),
        ],
        in_specs=[vmem] * 4,
        out_specs=[anywhere] * 3,
        scratch_shapes=[pltpu.VMEM((rows, columns), F32), pltpu.SemaphoreType.DMA((pieces + 2,))],
        compiler_params=pltpu.CompilerParams(vmem_limit_bytes=32 * 1024 * 1024),
    )(*outputs)
    return plan, row_potential.reshape(rows), col_potential.reshape(columns)


def solution(mesh):
    return jax.shard_map(
        per_device,
        mesh=mesh,
        in_specs=(
            P("row", "col"),
            P("row", None),
            P("row", None),
            P("row", "col"),
            P("row", "col"),
            P("row"),
            P("col"),
            P("col"),
        ),
        out_specs=(P("row", "col"), P("row"), P("col")),
        check_vma=False,
    )
```
